32 devices in a mesh: dp: 8 (over z, x), mp: 4 (over y, core).
Axes of the slice: x: 2, y: 2, z: 4, core: 2. Of those that a mesh axis runs over, the one named last changes fastest.
Arguments:
- tokens: bfloat16 [8192, 768], P('dp'), may hold values from -6 to 6
- lengths: int32 [16, 7], P('dp'), may hold values from 1 to 128, 512 in all within a row
- send_slot: int32 [96], P('dp'), may hold values from 0 to 15, as said below
- recv_place: int32 [128], P('dp'), may hold values from 0 to 12, as said below
- w_query: bfloat16 [768, 768], P(None, 'mp'), may hold values from -0.21875 to 0.21875
- b_query: float32 [768], P('mp'), may hold values from -3 to 3
- w_key: bfloat16 [768, 768], P(None, 'mp'), may hold values from -0.21875 to 0.21875
- w_value: bfloat16 [768, 768], P(None, 'mp'), may hold values from -0.21875 to 0.21875
- b_value: float32 [768], P('mp'), may hold values from -3 to 3
- w_out: bfloat16 [768, 768], P('mp'), may hold values from -1.25 to 1.25
- output_bias: float32 [768], replicated, may hold values from -3 to 3
- first_norm_gain: float32 [768], replicated, may hold values from 0.5 to 1.5
- first_norm_bias: float32 [768], replicated, may hold values from -1.75 to 1.75
- w_up: bfloat16 [768, 3072], P(None, 'mp'), may hold values from -0.21875 to 0.21875
- b_up: float32 [3072], P('mp'), may hold values from -3 to 3
- w_down: bfloat16 [3072, 768], P('mp'), may hold values from -0.109375 to 0.109375
- down_bias: float32 [768], replicated, may hold values from -3 to 3
- second_norm_gain: float32 [768], replicated, may hold values from 0.5 to 1.5
- second_norm_bias: float32 [768], replicated, may hold values from -0.3125 to 0.3125
- out_grad: bfloat16 [8192, 768], P('dp'), may hold values from -6 to 6
Outputs:
- result: bfloat16 [8192, 768], P('dp')
- pair_loss: float32 [48], P('dp')
- tokens_grad: float32 [8192, 768], P('dp')
- g_w_query: float32 [768, 768], P(None, 'mp')
- g_b_query: float32 [768], P('mp')
- g_w_key: float32 [768, 768], P(None, 'mp')
- g_w_value: float32 [768, 768], P(None, 'mp')
- g_b_value: float32 [768], P('mp')
- g_w_out: float32 [768, 768], P('mp')
- g_b_out: float32 [768], replicated
- first_gain_gradient: float32 [768], replicated
- g_bias_one: float32 [768], replicated
- g_w_up: float32 [768, 3072], P(None, 'mp')
- g_b_up: float32 [3072], P('mp')
- g_w_down: float32 [3072, 768], P('mp')
- g_b_down: float32 [768], replicated
- second_gain_gradient: float32 [768], replicated
- g_bias_two: float32 [768], replicated
The draws below stay inside these ranges and needn't reach their ends.
Inputs may be any that keep to these rules, and one draw needn't show every extreme that they name: `send_slot`: on each dp index the 12 entries are distinct send slots; slot // 2 is the dp index that receives the sentence; at most 2 sentences go from one index to another, and each index sends exactly 2 to some peer. `recv_place`: entry i * 2 + k of a dp index's block is the place, in that index's pair order, of the sentence that dp index i puts in send slot (this index) * 2 + k, as send_slot gives; each place 0 to 11 occurs once on every index, and slots that no sentence fills hold 12.
All inputs are finite; a program needn't handle non-finite values.
Results may differ from the reference program's by a relative error of at most 0.024.
Values may be sent and summed in bfloat16 or wider, within the bound.
A program may use at most 128 MiB of HBM per device.

```python
import math
import jax
import jax.numpy as jnp
import numpy as np
from jax import lax

D = 768
HEADS = 12
HEAD_DIM = 64
FF = 3072
SEQ = 512
SEG_ROW = 6
MAXLEN = 128
ROWS_DEV = 2
ROWS = 16
P_DEV = 12
PAIRS_DEV = 6
CAP = 2
N_DP = 8
N_MP = 4


def pair_layout(key):
    shift_key, send_key, place_key = jax.random.split(key, 3)
    shift_rank = jax.random.permutation(shift_key, N_DP).astype(jnp.int32)
    rank_index = jnp.arange(N_DP, dtype=jnp.int32)
    quota = jnp.where(rank_index % 2 == 0, CAP, CAP // 2).astype(jnp.int32)
    before = (jnp.cumsum(quota) - quota).astype(jnp.int32)
    amount_rank = jnp.clip(P_DEV - before, 0, quota).astype(jnp.int32)
    amount = amount_rank[shift_rank]
    device_index = jnp.arange(N_DP, dtype=jnp.int32)
    counts = amount[(device_index[None, :] - device_index[:, None]) % N_DP]
    slot_index = jnp.arange(N_DP * CAP, dtype=jnp.int32)
    slot_peer = slot_index // CAP
    slot_within = slot_index % CAP

    def send_one(source, sub_key):
        usable = slot_within < counts[source, slot_peer]
        order = jnp.argsort(jnp.where(usable, slot_index, slot_index + N_DP * CAP), stable=True)[:P_DEV]
        shuffle = jax.random.permutation(sub_key, P_DEV)
        return jnp.zeros((P_DEV,), jnp.int32).at[shuffle].set(order.astype(jnp.int32))

    def recv_one(target, sub_key):
        usable = slot_within < counts[slot_peer, target]
        order = jnp.argsort(jnp.where(usable, slot_index, slot_index + N_DP * CAP), stable=True)[:P_DEV]
        places = jax.random.permutation(sub_key, P_DEV).astype(jnp.int32)
        return jnp.full((N_DP * CAP,), P_DEV, jnp.int32).at[order].set(places)
    send_all = jax.vmap(send_one)(device_index, jax.random.split(send_key, N_DP))
    recv_all = jax.vmap(recv_one)(device_index, jax.random.split(place_key, N_DP))
    return (send_all.reshape(N_DP * P_DEV), recv_all.reshape(N_DP * N_DP * CAP))


def draw_send_slot(key, part):
    return pair_layout(jax.random.fold_in(key, 11))[0]


def draw_recv_place(key, part):
    return pair_layout(jax.random.fold_in(key, 11))[1]


def steps_of(rng, dims, cuts, low, largest):
    gain, own = 1.0, jax.random.fold_in(rng, 6)
    for dim, shards_of in cuts:
        steps = jnp.exp(jax.random.uniform(jax.random.fold_in(own, dim), (shards_of,), jnp.float32, low / len(cuts), largest / len(cuts)))
        gain = gain * jnp.repeat(steps, dims[dim] // shards_of).reshape([-1 if axis == dim else 1 for axis in range(len(dims))])
    return gain


def profile(number_of, total, most, skew):
    weights = [(1 << 20) // math.isqrt(rank ** skew) + 1 for rank in range(2, number_of + 1)]
    rest, given = total - most - (number_of - 1), [1] * (number_of - 1)
    while rest > 0:
        free = [i for i in range(number_of - 1) if given[i] < most]
        pool, budget = sum([weights[i] for i in free]), rest
        for i in free:
            extra = min(most - given[i], max(1, budget * weights[i] // pool), rest)
            given[i] = given[i] + extra
            rest = rest - extra
    return np.array([most] + given)


def uneven(key, number_of, total, most, skew):
    if number_of == 2:
        one = jax.random.randint(key, (), max(1, total - most), min(most, total - 1) + 1)
        return jnp.stack([one, total - one])
    tallies = jnp.asarray(profile(number_of, total, most, skew), jnp.int32)
    twos = (number_of - 1) // 2
    donor, sink = tallies[1:1 + 2 * twos:2], tallies[2:2 + 2 * twos:2]
    slack = jnp.minimum(donor - 1, most - sink)
    passed = jax.random.randint(jax.random.fold_in(key, 1), (twos,), 0, 1 << 20) % (slack + 1)
    tallies = tallies.at[1:1 + 2 * twos:2].set(donor - passed).at[2:2 + 2 * twos:2].set(sink + passed)
    return tallies[jax.random.permutation(jax.random.fold_in(key, 2), number_of)]


def centred(rng, dims, scale, reach, cuts=(), held_as=jnp.bfloat16):
    array = scale * jax.random.normal(rng, dims, jnp.float32)
    if cuts:
        array = array * steps_of(rng, dims, cuts, -0.22, 0.18)
    return jnp.clip(array, -reach, reach).astype(held_as)


def setup_inputs(seed: int = 0) -> dict:
    splits = jax.random.split(jax.random.key(seed), 21)
    tokens = centred(splits[0], (ROWS * SEQ, D), 1.0, 6.0, ((0, 8),))
    lengths = jax.vmap(lambda own: uneven(own, SEG_ROW + 1, SEQ, MAXLEN, 2))(jax.random.split(splits[1], ROWS)).reshape((ROWS, SEG_ROW + 1)).astype(jnp.int32)
    send_slot = draw_send_slot(jax.random.fold_in(splits[20], 71), 0)
    recv_place = draw_recv_place(jax.random.fold_in(splits[20], 71), 0)
    w_query = centred(splits[4], (D, D), D ** -0.5, 0.21875, ((1, 4),))
    b_query = centred(splits[5], (D,), 0.5, 3.0, ((0, 4),), jnp.float32)
    w_key = centred(splits[6], (D, D), D ** -0.5, 0.21875, ((1, 4),))
    w_value = centred(splits[7], (D, D), D ** -0.5, 0.21875, ((1, 4),))
    b_value = centred(splits[8], (D,), 0.5, 3.0, ((0, 4),), jnp.float32)
    w_out = centred(splits[9], (D, D), (max(4, D * MAXLEN // 4096)) ** -0.5, 1.25, ((0, 4),))
    output_bias = centred(splits[10], (D,), 0.5, 3.0, (), jnp.float32)
    first_norm_gain = jnp.clip(1.0 + 0.1 * jax.random.normal(splits[11], (D,), jnp.float32), 0.5, 1.5)
    first_norm_bias = centred(splits[12], (D,), 0.3, 1.75, (), jnp.float32)
    w_up = centred(splits[13], (D, FF), D ** -0.5, 0.21875, ((1, 4),))
    b_up = centred(splits[14], (FF,), 0.5, 3.0, ((0, 4),), jnp.float32)
    w_down = centred(splits[15], (FF, D), FF ** -0.5, 0.109375, ((0, 4),))
    down_bias = centred(splits[16], (D,), 0.5, 3.0, (), jnp.float32)
    second_norm_gain = jnp.clip(1.0 + 0.1 * jax.random.normal(splits[17], (D,), jnp.float32), 0.5, 1.5)
    second_norm_bias = centred(splits[18], (D,), 0.05, 0.3125, (), jnp.float32)
    out_grad = centred(splits[19], (ROWS * SEQ, D), 1.0, 6.0, ((0, 8),))
    return dict(tokens=tokens, lengths=lengths, send_slot=send_slot, recv_place=recv_place, w_query=w_query, b_query=b_query, w_key=w_key, w_value=w_value, b_value=b_value, w_out=w_out, output_bias=output_bias, first_norm_gain=first_norm_gain, first_norm_bias=first_norm_bias, w_up=w_up, b_up=b_up, w_down=w_down, down_bias=down_bias, second_norm_gain=second_norm_gain, second_norm_bias=second_norm_bias, out_grad=out_grad)


NEG_FILL = -1e+30
NORM_EPS = 1e-12
UNIT_EPS = 1e-06
SIM_SCALE = 50.0
HIGHEST = lax.Precision.HIGHEST

@jax.custom_vjp
def low(v):
    return lax.optimization_barrier(v.astype(jnp.bfloat16)).astype(jnp.float32)

@jax.custom_vjp
def low_back(v):
    return v

def low_keep(v):
    return (low(v), None)

def low_pass(kept, upstream_gradient):
    return (upstream_gradient,)

def back_keep(v):
    return (v, None)

def back_low(kept, upstream_gradient):
    return (low(upstream_gradient),)
low.defvjp(low_keep, low_pass)
low_back.defvjp(back_keep, back_low)

def matmul(left, right):
    return jnp.dot(left, right, precision=HIGHEST, preferred_element_type=jnp.float32)

def normalize(hidden_state):
    middle = lax.optimization_barrier(jnp.mean(hidden_state, axis=-1, keepdims=True))
    centered = hidden_state - middle
    spread = lax.optimization_barrier(jnp.mean(centered * centered, axis=-1, keepdims=True))
    return centered * lax.rsqrt(spread + NORM_EPS)

def segment_tables(lengths, seq_len):
    ends = jnp.cumsum(lengths, axis=1).astype(jnp.int32)
    starts = ends - lengths
    position = jnp.arange(seq_len, dtype=jnp.int32)
    member = (position[None, None, :] >= starts[:, :, None]) & (position[None, None, :] < ends[:, :, None])
    seg_id = lax.optimization_barrier(jnp.sum((position[None, None, :] >= ends[:, :, None]).astype(jnp.int32), axis=1))
    return (member, seg_id)

def score_pairs(ordered):
    anchors = ordered[:, 0, :]
    positives = ordered[:, 1, :]
    anchor_unit = anchors * lax.rsqrt(lax.optimization_barrier(jnp.sum(anchors * anchors, axis=-1, keepdims=True)) + UNIT_EPS)
    positive_unit = positives * lax.rsqrt(lax.optimization_barrier(jnp.sum(positives * positives, axis=-1, keepdims=True)) + UNIT_EPS)
    logits = SIM_SCALE * lax.dot_general(anchor_unit, positive_unit, (((1,), (1,)), ((), ())), precision=HIGHEST, preferred_element_type=jnp.float32)
    peak = lax.optimization_barrier(jnp.max(logits, axis=-1, keepdims=True))
    log_total = peak[:, 0] + jnp.log(lax.optimization_barrier(jnp.sum(jnp.exp(logits - peak), axis=-1)))
    return log_total - jnp.diagonal(logits)

def group_forward(params, tokens_f, lengths_g):
    w_query, b_query, w_key, w_value, b_value, w_out, output_bias, first_norm_gain, first_norm_bias, w_up, b_up, w_down, down_bias, second_norm_gain, second_norm_bias = params
    row_count = lengths_g.shape[0]
    token_count = tokens_f.shape[0]
    seq_len = token_count // row_count
    member, seg_id = segment_tables(lengths_g, seq_len)
    same_piece = seg_id[:, :, None] == seg_id[:, None, :]
    local_width = D // N_MP
    head_group = HEADS // N_MP
    hidden_group = FF // N_MP
    scale = HEAD_DIM ** (-0.5)
    shaped = (row_count, seq_len, head_group, HEAD_DIM)
    attention_grand_total = jnp.zeros((token_count, D), jnp.float32)
    for group in range(N_MP):
        columns = slice(group * local_width, (group + 1) * local_width)
        tokens_g = low_back(tokens_f)
        query_rows = low_back(low(matmul(tokens_g, w_query[:, columns]) + b_query[columns])).reshape(shaped)
        key_rows = low_back(low(matmul(tokens_g, w_key[:, columns]))).reshape(shaped)
        value_rows = low_back(low(matmul(tokens_g, w_value[:, columns]) + b_value[columns])).reshape(shaped)
        raw_scores = jnp.einsum('rqhd,rkhd->rhqk', query_rows, key_rows, precision=HIGHEST)
        scores = jnp.where(same_piece[:, None], low_back(raw_scores) * scale, NEG_FILL)
        peak = lax.optimization_barrier(jnp.max(scores, axis=-1, keepdims=True))
        exponent = jnp.exp(scores - peak)
        probs = low(exponent / lax.optimization_barrier(jnp.sum(exponent, axis=-1, keepdims=True)))
        context_rows = jnp.einsum('rhqk,rkhd->rqhd', probs, value_rows, precision=HIGHEST)
        context_rows = low_back(low(context_rows)).reshape(token_count, local_width)
        attention_grand_total = attention_grand_total + low(low_back(matmul(context_rows, w_out[columns, :])))
    hidden_state = normalize(tokens_f + attention_grand_total + output_bias) * first_norm_gain + first_norm_bias
    hidden_low = low(hidden_state)
    feedforward_grand_total = jnp.zeros((token_count, D), jnp.float32)
    for group in range(N_MP):
        units = slice(group * hidden_group, (group + 1) * hidden_group)
        hidden_g = low_back(hidden_low)
        up_value = low_back(matmul(hidden_g, w_up[:, units]) + b_up[units])
        active = low_back(low(jax.nn.gelu(up_value, approximate=False)))
        feedforward_grand_total = feedforward_grand_total + low(low_back(matmul(active, w_down[units, :])))
    result = normalize(hidden_state + feedforward_grand_total + down_bias) * second_norm_gain + second_norm_bias
    chosen = member[:, :-1].astype(jnp.float32)
    sent_sizes = lengths_g[:, :-1].astype(jnp.float32)
    pooled = jnp.einsum('rpt,rtd->rpd', chosen, result.reshape(row_count, seq_len, D), precision=HIGHEST) / sent_sizes[:, :, None]
    pooled = low_back(low(pooled.reshape(row_count * (lengths_g.shape[1] - 1), D)))
    return (result, pooled)

def forward(params, tokens_f, lengths, send_slot, recv_place):
    groups_x = tokens_f.reshape(N_DP, ROWS_DEV * SEQ, D)
    groups_len = lengths.reshape(N_DP, ROWS_DEV, SEG_ROW + 1)

    def scan_step(carry, item):
        return (carry, group_forward(params, item[0], item[1]))
    _, (result, pooled) = lax.scan(jax.checkpoint(scan_step), jnp.zeros((), jnp.float32), (groups_x, groups_len))
    pooled = pooled.reshape(N_DP * P_DEV, D)
    source = jnp.arange(N_DP * P_DEV, dtype=jnp.int32) // P_DEV
    target_dev = send_slot // CAP
    within = send_slot % CAP
    receive = target_dev * (N_DP * CAP) + source * CAP + within
    place = recv_place[receive]
    target = target_dev * P_DEV + place
    ordered = jnp.zeros((N_DP * P_DEV, D), jnp.float32).at[target].set(pooled)
    pair_loss = jax.vmap(score_pairs)(ordered.reshape(N_DP, PAIRS_DEV, 2, D)).reshape(N_DP * PAIRS_DEV)
    return (result.reshape(N_DP * ROWS_DEV * SEQ, D), pair_loss)

def reference(tokens, lengths, send_slot, recv_place, w_query, b_query, w_key, w_value, b_value, w_out, output_bias, first_norm_gain, first_norm_bias, w_up, b_up, w_down, down_bias, second_norm_gain, second_norm_bias, out_grad):
    params = tuple((weight.astype(jnp.float32) for weight in (w_query, b_query, w_key, w_value, b_value, w_out, output_bias, first_norm_gain, first_norm_bias, w_up, b_up, w_down, down_bias, second_norm_gain, second_norm_bias)))
    tokens_f = tokens.astype(jnp.float32)

    def objective(params_f, tokens_v):
        return forward(params_f, tokens_v, lengths, send_slot, recv_place)
    (result, pair_loss), pullback = jax.vjp(objective, params, tokens_f)
    grads, tokens_grad = pullback((out_grad.astype(jnp.float32), jnp.ones_like(pair_loss)))
    return (result.astype(jnp.bfloat16), pair_loss, tokens_grad, grads[0], grads[1], grads[2], grads[3], grads[4], grads[5], grads[6], grads[7], grads[8], grads[9], grads[10], grads[11], grads[12], grads[13], grads[14])
```

```python
import functools

import jax
import jax.numpy as jnp
from jax import lax
from jax.experimental import pallas as pl
from jax.experimental.pallas import tpu as pltpu
from jax.sharding import PartitionSpec as P

HEAD_DIM = 64
MAX_PIECE = 128
NEG_FILL = -1e30
NORM_EPS = 1e-12
UNIT_EPS = 1e-06
SIM_SCALE = 50.0
MESH = pl.DeviceIdType.MESH
F32, BF16, I32 = jnp.float32, jnp.bfloat16, jnp.int32
HIGHEST = lax.Precision.HIGHEST


def nn(a, b):
    return lax.dot_general(a, b, (((1,), (0,)), ((), ())), preferred_element_type=F32)


def nt(a, b):
    return lax.dot_general(a, b, (((1,), (1,)), ((), ())), preferred_element_type=F32)


def tn(a, b):
    return lax.dot_general(a, b, (((0,), (0,)), ((), ())), preferred_element_type=F32)


def iota(shape, axis):
    return lax.broadcasted_iota(I32, shape, axis)


def hi_lo(x):
    hi = x.astype(BF16).astype(F32)
    return hi, x - hi


def sizes(n_dp, rows, tokens, width, local, hidden):
    return dict(
        n_dp=n_dp, R=rows, T=tokens, S=tokens // rows, D=width, L=local, F=hidden,
        half=tokens // rows // 2, heads=local // HEAD_DIM,
    )


def layer_kernel(z, names, *refs):
    ref = dict(zip(names, refs))
    g = lambda k: ref[k]
    n_dp, R, S, D, L, F, half, heads = (
        z[k] for k in ("n_dp", "R", "S", "D", "L", "F", "half", "heads")
    )
    T = R * S
    QB = 256 if S % 256 == 0 else S
    n_qb = S // QB
    KB = QB + MAX_PIECE
    CH = D // 128
    dp, mp = lax.axis_index("dp"), lax.axis_index("mp")
    core = mp % 2
    other = 1 - core
    sib = (dp, mp + 1 - 2 * core)
    across = (dp, (mp + 2) % 4)

    bar = pltpu.get_barrier_semaphore()
    for t in (sib, across):
        pl.semaphore_signal(bar, inc=1, device_id=t, device_id_type=MESH)
    for d in range(1, n_dp):
        pl.semaphore_signal(bar, inc=1, device_id=((dp + d) % n_dp, mp), device_id_type=MESH)

    loads = {}
    for i, k in enumerate(("tokens", "wq", "wk", "wv", "wo", "wu", "wd", "og")):
        c = pltpu.make_async_copy(g(k), g(k + "_v"), g("in_sem").at[i])
        c.start()
        loads[k] = c
    pl.semaphore_wait(bar, 1 + n_dp)

    sends = []

    def remote(src, dst, ss, rs, to):
        return pltpu.make_async_remote_copy(
            src_ref=src, dst_ref=dst, send_sem=ss, recv_sem=rs, device_id=to, device_id_type=MESH
        )

    vecs = g("vecs")

    def vec(i, n=None):
        return vecs[i : i + 1, : (n or D)]

    ends = []
    for r in range(R):
        total, row = 0, []
        for p in range(7):
            total = total + g("lengths")[r, p]
            row.append(total)
        ends.append(row)

    def seg_of(position, r):
        seg = jnp.zeros(position.shape, I32)
        for p in range(6):
            seg = seg + jnp.where(position >= ends[r][p], 1, 0)
        return seg

    lane_head = iota((1, L), 1) // HEAD_DIM

    def only_head(x, h):
        return jnp.where(lane_head == h, x, jnp.zeros_like(x))

    def send_half(which, r, compute):
        par = which % 2
        if which >= 2:
            remote(g("asend").at[par, r], g("arecv").at[par, r], g("a_s").at[which - 2, r],
                   g("a_r").at[which - 2, r], sib).wait_send()
        compute(other * half, lambda cols, val: g("asend").__setitem__((par, r, slice(None), cols), val.astype(BF16)))
        c = remote(g("asend").at[par, r], g("arecv").at[par, r], g("a_s").at[which, r], g("a_r").at[which, r], sib)
        c.start()
        compute(core * half, lambda cols, val: g("own").__setitem__((r, slice(None), cols), val))
        if which >= 2:
            sends.append(c)
        return c

    def send_across(which, r, c):
        par = which % 2
        c.wait_recv()
        if which >= 2:
            remote(g("ysend").at[par, r], g("yrecv").at[par, r], g("y_s").at[which - 2, r],
                   g("y_r").at[which - 2, r], across).wait_send()

        def add(i, _):
            rows = pl.ds(pl.multiple_of(i * 64, 64), 64)
            g("ysend")[par, r, rows] = (
                g("own")[r, rows].astype(F32) + g("arecv")[par, r, rows].astype(F32)
            ).astype(BF16)
            return 0

        lax.fori_loop(0, half // 64, add, 0)
        y = remote(g("ysend").at[par, r], g("yrecv").at[par, r], g("y_s").at[which, r], g("y_r").at[which, r], across)
        y.start()
        if which >= 2:
            sends.append(y)
        return y

    def y_total(which, r, rows):
        par = which % 2
        return g("ysend")[par, r, rows].astype(F32) + g("yrecv")[par, r, rows].astype(F32)

    def to_sibling(key, r, i):
        rows = pl.ds(pl.multiple_of(r * S + core * half, half), half)
        c = remote(g(key).at[rows], g(key).at[rows], g("g_s").at[i, r], g("g_r").at[i, r], sib)
        c.start()
        sends.append(c)
        return c

    TR = 32

    def by_rows(fn):
        def body(i, _):
            fn(pl.ds(pl.multiple_of(i * TR, TR), TR), i * TR)
            return 0

        lax.fori_loop(0, half // TR, body, 0)

    def fold(x):
        return jnp.sum(x.reshape(x.shape[0] // 8, 8, x.shape[1]), axis=0)

    def row_ds(r, start, n):
        return pl.ds(pl.multiple_of(r * S + core * half + start, TR), n)

    def project(r):
        rows = pl.ds(r * S, S)
        x = g("tokens_v")[rows, :]
        g("q")[rows, :] = ((nn(x, g("wq_v")[...]) + vec(0, L)).astype(BF16) * (HEAD_DIM**-0.5)).astype(BF16)
        g("k")[rows, :] = nn(x, g("wk_v")[...]).astype(BF16)
        g("v")[rows, :] = (nn(x, g("wv_v")[...]) + vec(1, L)).astype(BF16)

    def window(b):
        return min(max(b * QB - MAX_PIECE, 0), S - KB) if KB < S else 0

    KW = min(KB, S)
    if n_qb > 2:
        KW = min(QB + 2 * MAX_PIECE, S)

    def win(b):
        return min(max(b * QB - MAX_PIECE, 0), S - KW)

    def attend(r):
        for b in range(n_qb):
            q0, k0 = r * S + b * QB, r * S + win(b)
            same = seg_of(iota((QB, 1), 0) + b * QB, r) == seg_of(iota((1, KW), 1) + win(b), r)
            qb = g("q")[q0 : q0 + QB, :]
            kb = g("k")[k0 : k0 + KW, :]
            vb = g("v")[k0 : k0 + KW, :]
            ctx = None
            for h in range(heads):
                s = jnp.where(same, nt(only_head(qb, h), kb), NEG_FILL)
                e = jnp.exp(s - jnp.max(s, axis=-1, keepdims=True))
                p = (e * (1.0 / jnp.sum(e, axis=-1, keepdims=True))).astype(BF16)
                g("probs")[(r * n_qb + b) * heads + h] = p
                c = nn(p, only_head(vb, h))
                ctx = c if ctx is None else ctx + c
            g("ctx")[q0 : q0 + QB, :] = ctx.astype(BF16)

    def attn_out(r):
        def compute(start, put):
            x = g("ctx")[pl.ds(pl.multiple_of(r * S + start, half), half), :]
            for n in range(D // 256):
                put(slice(n * 256, n * 256 + 256), nn(x, g("wo_v")[:, n * 256 : n * 256 + 256]))

        return compute

    def norm(v):
        mean = jnp.mean(v, axis=-1, keepdims=True)
        c = v - mean
        rstd = lax.rsqrt(jnp.mean(c * c, axis=-1, keepdims=True) + NORM_EPS)
        return c * rstd, rstd

    def first_norm(r):
        def body(rows, start):
            mine = row_ds(r, start, TR)
            xh, rstd = norm(g("tokens_v")[mine].astype(F32) + y_total(0, r, rows) + vec(2))
            g("xhat1")[r, rows] = xh
            g("rstd1")[r, rows] = rstd
            h = xh * vec(3) + vec(4)
            g("hid")[r, rows] = h
            g("hl")[mine] = h.astype(BF16)

        by_rows(body)

    FM = 256
    FT = 256

    def ffn_up(r):
        def body(i, _):
            rows = pl.ds(pl.multiple_of(r * S + i * FM, FM), FM)
            x = g("hl")[rows, :]
            for n in range(F // FT):
                cols = slice(n * FT, n * FT + FT)
                u = nn(x, g("wu_v")[:, cols]) + vecs[5:6, cols]
                phi = 0.5 + 0.5 * lax.erf(u * 0.7071067811865476)
                g("act")[rows, cols] = (u * phi).astype(BF16)
                g("gp")[rows, cols] = (phi + u * (jnp.exp(-0.5 * (u * u)) * 0.3989422804014327)).astype(BF16)
            return 0

        lax.fori_loop(0, S // FM, body, 0)

    def ffn_down(r):
        def compute(start, put):
            x = g("act")[pl.ds(pl.multiple_of(r * S + start, half), half), :]
            for n in range(D // 256):
                put(slice(n * 256, n * 256 + 256), nn(x, g("wd_v")[:, n * 256 : n * 256 + 256]))

        return compute

    def second_norm(r):
        lane = iota((8, TR), 1)
        piece = iota((8, TR), 0)

        def body(rows, start):
            xh, rstd = norm(g("hid")[r, rows] + y_total(1, r, rows) + vec(6))
            g("xhat2")[r, rows] = xh
            g("rstd2")[r, rows] = rstd
            res = xh * vec(7) + vec(8)
            low = res.astype(BF16)
            g("res")[row_ds(r, start, TR)] = low
            seg = seg_of(lane + (core * half + start), r)
            member = jnp.where((seg == piece) & (piece < 6), 1.0, 0.0).astype(BF16)
            rest = (res - low.astype(F32)).astype(BF16)
            at = slice(r * 8, r * 8 + 8)
            g("pool")[at, :] = g("pool")[at, :] + nn(member, low) + nn(member, rest)

        by_rows(body)

    PR = 16
    n_sent = R * 6

    def per_row(values, axis, shape, fill):
        pos = iota(shape, axis) % PR
        out = jnp.full(shape, fill, I32)
        for s in range(n_sent):
            out = jnp.where(pos == (s // 6) * 8 + s % 6, values[s], out)
        return out

    def slot_onehot(axis):
        shape = (n_dp * 16, CH * PR) if axis == 1 else (CH * PR, n_dp * 16)
        line = (1, CH * PR) if axis == 1 else (CH * PR, 1)
        vals = [g("send_slot")[s] // 2 * 16 + g("send_slot")[s] % 2 for s in range(n_sent)]
        target = per_row(vals, axis if axis == 1 else 0, line, -65536) + iota(line, 1 if axis == 1 else 0) // PR * 2
        return jnp.where(iota(shape, 0 if axis == 1 else 1) == target, 1.0, 0.0).astype(BF16)

    def place_onehot(axis):
        line = (1, n_dp * 16) if axis == 1 else (n_dp * 16, 1)
        shape = (CH * PR, n_dp * 16) if axis == 1 else (n_dp * 16, CH * PR)
        pos = iota(line, axis)
        slot = pos // 16 * 2 + pos % 2
        target = jnp.zeros(line, I32)
        for s in range(2 * n_dp):
            target = jnp.where(slot == s, g("recv_place")[s], target)
        target = target + pos % 16 // 2 * PR
        return jnp.where(iota(shape, 0 if axis == 1 else 1) == target, 1.0, 0.0).astype(BF16)

    def stack(x):
        return jnp.concatenate([x[:, c * 128 : c * 128 + 128] for c in range(CH)], axis=0)

    def unstack(x):
        return jnp.concatenate([x[c * PR : c * PR + PR] for c in range(CH)], axis=1)

    def peers(src, dst, ssem, rsem):
        cs = []
        mine = pl.ds(pl.multiple_of(dp * 16, 16), 16)
        for d in range(1, n_dp):
            t = (dp + d) % n_dp
            c = remote(src.at[pl.ds(pl.multiple_of(t * 16, 16), 16)], dst.at[mine], ssem.at[d], rsem.at[d], (t, mp))
            c.start()
            cs.append(c)
            sends.append(c)
        dst[mine] = src[mine]
        for c in cs:
            c.wait_recv()

    def pairs():
        c = remote(g("pool"), g("pool_r"), g("pool_sem").at[0], g("pool_sem").at[1], sib)
        c.start()
        lens = [g("lengths")[s // 6, s % 6] for s in range(n_sent)]
        size = per_row(lens, 0, (PR, 1), 1).astype(F32)
        inv = 1.0 / size
        hot = slot_onehot(1)
        c.wait()
        pooled = (g("pool")[...] + g("pool_r")[...]) * inv
        g("outg")[...] = nn(hot, stack(pooled).astype(BF16)).astype(BF16)
        peers(g("outg"), g("inc"), g("p_s").at[0], g("p_r").at[0])
        o = unstack(nn(place_onehot(1), g("inc")[...]))
        s = lax.rsqrt(jnp.sum(o * o, axis=-1, keepdims=True) + UNIT_EPS)
        u = o * s
        logits = SIM_SCALE * lax.dot_general(
            u, u, (((1,), (1,)), ((), ())), precision=HIGHEST, preferred_element_type=F32
        )
        i, j = iota((PR, PR), 0), iota((PR, PR), 1)
        live = (i % 2 == 0) & (i < n_sent) & (j % 2 == 1) & (j < n_sent)
        lm = jnp.where(live, logits, NEG_FILL)
        peak = jnp.max(lm, axis=-1, keepdims=True)
        e = jnp.where(live, jnp.exp(lm - peak), 0.0)
        tot = jnp.maximum(jnp.sum(e, axis=-1, keepdims=True), 1e-30)
        partner = live & (j == i + 1)
        loss = peak + jnp.log(tot) - jnp.sum(jnp.where(partner, logits, 0.0), axis=-1, keepdims=True)
        i2, j2 = iota((PR, 128), 0), iota((PR, 128), 1)
        g("loss_v")[...] = jnp.broadcast_to(
            jnp.sum(jnp.where((i2 == 2 * j2) & (i2 < n_sent), loss, 0.0), axis=0, keepdims=True), (8, 128)
        )
        dl = e / tot - jnp.where(partner, 1.0, 0.0)
        du = SIM_SCALE * (
            lax.dot_general(dl, u, (((1,), (0,)), ((), ())), precision=HIGHEST, preferred_element_type=F32)
            + lax.dot_general(dl, u, (((0,), (0,)), ((), ())), precision=HIGHEST, preferred_element_type=F32)
        )
        do = s * (du - u * jnp.sum(u * du, axis=-1, keepdims=True))
        g("outg2")[...] = nn(place_onehot(0), stack(do).astype(BF16)).astype(BF16)
        peers(g("outg2"), g("inc2"), g("p_s").at[1], g("p_r").at[1])
        g("dpool")[...] = unstack(nn(slot_onehot(0), g("inc2")[...])) * inv

    def norm_back(dx, xh, rstd):
        return rstd * (
            dx - jnp.mean(dx, axis=-1, keepdims=True) - xh * jnp.mean(dx * xh, axis=-1, keepdims=True)
        )

    def second_norm_back(r):
        hi, lo = hi_lo(g("dpool")[r * 8 : r * 8 + 8, :])
        rhs = jnp.concatenate([hi, lo], axis=0).astype(BF16)
        lane = iota((TR, 16), 1) % 8

        def body(rows, start):
            mine = row_ds(r, start, TR)
            seg = seg_of(iota((TR, 1), 0) + (core * half + start), r)
            member = jnp.where((seg == lane) & (lane < 6), 1.0, 0.0).astype(BF16)
            d = g("og_v")[mine].astype(F32) + nn(member, rhs)
            xh = g("xhat2")[r, rows]
            g("acc")[4] += fold(d * xh)
            g("acc")[5] += fold(d)
            d2 = norm_back(d * vec(7), xh, g("rstd2")[r, rows])
            g("acc")[3] += fold(d2)
            g("d2")[r, rows] = d2
            g("d2l")[mine] = d2.astype(BF16)

        by_rows(body)

    def ffn_back(r):
        def body(i, _):
            rows = pl.ds(pl.multiple_of(r * S + i * FM, FM), FM)
            x = g("d2l")[rows, :]
            for n in range(F // FT):
                cols = slice(n * FT, n * FT + FT)
                da = nt(x, g("wd_v")[cols, :]).astype(BF16)
                du = (da.astype(F32) * g("gp")[rows, cols].astype(F32)).astype(BF16)
                g("dup")[rows, cols] = du
                g("acc")[6, :, cols] += fold(du.astype(F32))
            return 0

        lax.fori_loop(0, S // FM, body, 0)

    def ffn_back_out(r):
        def compute(start, put):
            x = g("dup")[pl.ds(pl.multiple_of(r * S + start, half), half), :]
            for n in range(D // 256):
                put(slice(n * 256, n * 256 + 256), nt(x, g("wu_v")[n * 256 : n * 256 + 256, :]))

        return compute

    def ffn_weights():
        for n in range(F // 256):
            g("grad")[0, n * 256 : n * 256 + 256, :] = tn(g("act")[:, n * 256 : n * 256 + 256], g("d2l")[...]).astype(BF16)
        for n in range(D // 256):
            g("grad")[1, n * 256 : n * 256 + 256, :] = tn(g("hl")[:, n * 256 : n * 256 + 256], g("dup")[...]).astype(BF16)

    def first_norm_back(r):
        def body(rows, start):
            mine = row_ds(r, start, TR)
            d = g("d2")[r, rows] + y_total(2, r, rows)
            xh = g("xhat1")[r, rows]
            g("acc")[1] += fold(d * xh)
            g("acc")[2] += fold(d)
            d1 = norm_back(d * vec(3), xh, g("rstd1")[r, rows])
            g("acc")[0] += fold(d1)
            g("d1")[r, rows] = d1
            g("d1l")[mine] = d1.astype(BF16)

        by_rows(body)

    def attend_back(r):
        rows = pl.ds(r * S, S)
        g("dctx")[rows, :] = nt(g("d1l")[rows, :], g("wo_v")[...]).astype(BF16)
        g("dk_acc")[...] = jnp.zeros((S, L), F32)
        g("dv_acc")[...] = jnp.zeros((S, L), F32)
        for b in range(n_qb):
            q0, k0 = r * S + b * QB, r * S + win(b)
            qb = g("q")[q0 : q0 + QB, :]
            cb = g("dctx")[q0 : q0 + QB, :]
            kb = g("k")[k0 : k0 + KW, :]
            vb = g("v")[k0 : k0 + KW, :]
            dq = dk = dv = None
            for h in range(heads):
                p = g("probs")[(r * n_qb + b) * heads + h]
                dp_ = nt(cb, only_head(vb, h))
                pf = p.astype(F32)
                delta = jnp.sum(pf * dp_, axis=-1, keepdims=True)
                ds = (pf * (dp_ - delta)).astype(BF16)
                a, c, e = nn(ds, only_head(kb, h)), tn(ds, only_head(qb, h)), tn(p, only_head(cb, h))
                dq, dk, dv = (a, c, e) if dq is None else (dq + a, dk + c, dv + e)
            g("dq")[q0 : q0 + QB, :] = (dq * (HEAD_DIM**-0.5)).astype(BF16)
            g("dk_acc")[win(b) : win(b) + KW, :] += dk
            g("dv_acc")[win(b) : win(b) + KW, :] += dv
        g("dk")[rows, :] = g("dk_acc")[...].astype(BF16)
        g("dv")[rows, :] = g("dv_acc")[...].astype(BF16)
        g("acc")[7, :, :L] += fold(g("dq")[rows, :].astype(F32))
        g("acc")[8, :, :L] += fold(g("dv")[rows, :].astype(F32))

    def attend_back_out(r):
        def compute(start, put):
            at = pl.ds(pl.multiple_of(r * S + start, half), half)
            for n in range(D // 256):
                w = slice(n * 256, n * 256 + 256)
                put(
                    w,
                    nt(g("dq")[at, :], g("wq_v")[w, :])
                    + nt(g("dk")[at, :], g("wk_v")[w, :])
                    + nt(g("dv")[at, :], g("wv_v")[w, :]),
                )

        return compute

    def attend_weights():
        for i, k in enumerate(("dq", "dk", "dv")):
            g("grad")[2, i * L : i * L + L, :] = tn(g(k)[...], g("tokens_v")[...]).astype(BF16)
        g("grad")[2, 3 * L : 4 * L, :] = tn(g("ctx")[...], g("d1l")[...]).astype(BF16)

    def finish(r):
        def body(rows, start):
            g("tg")[row_ds(r, start, TR)] = g("d1")[r, rows] + y_total(3, r, rows)

        by_rows(body)

    xi, zi = dp % 2, dp // 2
    nz = n_dp // 2
    in_kernel = z["in_kernel"]
    outer = (zi == 0) | (zi == nz - 1)
    inner = (zi != 0) & (zi != nz - 1)
    xp = (dp + 1 - 2 * xi, mp)
    zp = (dp + 2 - 4 * (zi % 2), mp)
    zq = ((dp + 2 * (3 - 2 * zi)) % n_dp if in_kernel else dp, mp)
    ii = zi // 2
    grad, gsum = g("grad"), g("gsum")

    def add_into(dst, dst_at, a, a_at, b, b_at, n):
        step = 48 if n % 48 == 0 else 16

        def body(i, _):
            o = i * step
            x = a[a_at[0], pl.ds(pl.multiple_of(a_at[1] + o, 16), step), :].astype(F32)
            y = b[b_at[0], pl.ds(pl.multiple_of(b_at[1] + o, 16), step), :].astype(F32)
            dst[dst_at[0], pl.ds(pl.multiple_of(dst_at[1] + o, 16), step), :] = (x + y).astype(BF16)
            return 0

        lax.fori_loop(0, n // step, body, 0)

    def x_job(slot, j, r0, n):
        h = n // 2
        mine = pl.multiple_of(r0 + xi * h, 16)
        yours = pl.multiple_of(r0 + (1 - xi) * h, 16)
        own, theirs = pl.ds(mine, h), pl.ds(yours, h)
        s = lambda k: g("d_s").at[slot, k]
        q = lambda k: g("d_r").at[slot, k]
        buf = g("rx")
        x1 = remote(grad.at[j, theirs], buf.at[slot * 3], s(0), q(0), xp)
        z1 = remote(grad.at[j, own], buf.at[slot * 3 + 1], s(1), q(1), zp)
        z2 = remote(grad.at[j, own], buf.at[slot * 3 + 2], s(2), q(2), zq)
        z3 = remote(gsum.at[j, own], gsum.at[j, own], s(3), q(3), zp)
        x2 = remote(gsum.at[j, own], gsum.at[j, own], s(4), q(4), xp)

        def st0():
            x1.start()

        def st1():
            x1.wait_recv()
            add_into(grad, (j, mine), grad, (j, mine), buf, (slot * 3, 0), h)
            pl.when(outer)(z1.start)

        def st2():
            @pl.when(inner)
            def _():
                z1.wait_recv()
                add_into(grad, (j, mine), grad, (j, mine), buf, (slot * 3 + 1, 0), h)
                z2.start()

        def st3():
            @pl.when(inner)
            def _():
                z2.wait_recv()
                add_into(gsum, (j, mine), grad, (j, mine), buf, (slot * 3 + 2, 0), h)
                z3.start()
                x2.start()

        def st4():
            @pl.when(outer)
            def _():
                z3.wait_recv()
                x2.start()

        def st5():
            x2.wait_recv()

        def end():
            x1.wait_send()
            x2.wait_send()

            @pl.when(outer)
            def _():
                z1.wait_send()

            @pl.when(inner)
            def _():
                z2.wait_send()
                z3.wait_send()

        return [st0, st1, st2, st3, st4, st5], end

    def z_job(slot, j, r0, n):
        h = n // 2
        mine = pl.multiple_of(r0 + ii * h, 16)
        yours = pl.multiple_of(r0 + (1 - ii) * h, 16)
        own, theirs, whole = pl.ds(mine, h), pl.ds(yours, h), pl.ds(r0, n)
        s = lambda k: g("d_s").at[slot, k]
        q = lambda k: g("d_r").at[slot, k]
        buf, big = g("rx"), g("rz")
        z1 = remote(grad.at[j, whole], big.at[slot], s(0), q(0), zp)
        z2 = remote(grad.at[j, theirs], buf.at[slot * 3], s(1), q(1), zq)
        x = remote(grad.at[j, own], buf.at[slot * 3 + 1], s(2), q(2), xp)
        z2b = remote(gsum.at[j, own], gsum.at[j, own], s(3), q(3), zq)
        z3a = remote(gsum.at[j, own], gsum.at[j, own], s(4), q(4), zp)
        z3b = remote(gsum.at[j, theirs], gsum.at[j, theirs], s(5), q(5), zp)

        def st0():
            pl.when(outer)(z1.start)

        def st1():
            @pl.when(inner)
            def _():
                z1.wait_recv()
                add_into(grad, (j, r0), grad, (j, r0), big, (slot, 0), n)
                z2.start()

        def st2():
            @pl.when(inner)
            def _():
                z2.wait_recv()
                add_into(grad, (j, mine), grad, (j, mine), buf, (slot * 3, 0), h)
                x.start()

        def st3():
            @pl.when(inner)
            def _():
                x.wait_recv()
                add_into(gsum, (j, mine), grad, (j, mine), buf, (slot * 3 + 1, 0), h)
                z2b.start()
                z3a.start()

        def st4():
            @pl.when(inner)
            def _():
                z2b.wait_recv()
                z3b.start()

        def st5():
            @pl.when(outer)
            def _():
                z3a.wait_recv()
                z3b.wait_recv()

        def end():
            @pl.when(outer)
            def _():
                z1.wait_send()

            @pl.when(inner)
            def _():
                for c in (z2, x, z2b, z3a, z3b):
                    c.wait_send()

        return [st0, st1, st2, st3, st4, st5], end

    n_sub = z["n_sub"]
    sub = D // n_sub

    def jobs_of(j):
        made = []
        for i in range(n_sub):
            kind = x_job if i % 2 == 0 else z_job
            made.append(kind(j * n_sub + i, j, i * sub, sub))
        return made

    g("pool")[...] = jnp.zeros((PR, D), F32)
    g("acc")[...] = jnp.zeros(g("acc").shape, F32)
    for k in ("tokens", "wq", "wk", "wv"):
        loads[k].wait()
    a, y = {}, {}
    for r in range(R):
        project(r)
        attend(r)
        if r == 0:
            loads["wo"].wait()
        if r > 0:
            y[0, r - 1] = send_across(0, r - 1, a[0, r - 1])
        a[0, r] = send_half(0, r, attn_out(r))
    y[0, R - 1] = send_across(0, R - 1, a[0, R - 1])
    for k in ("wu", "wd", "og"):
        loads[k].wait()
    for r in range(R):
        y[0, r].wait_recv()
        first_norm(r)
        c = to_sibling("hl", r, 0)
        if r > 0:
            y[1, r - 1] = send_across(1, r - 1, a[1, r - 1])
        c.wait_recv()
        ffn_up(r)
        a[1, r] = send_half(1, r, ffn_down(r))
    y[1, R - 1] = send_across(1, R - 1, a[1, R - 1])
    out_c = []
    for r in range(R):
        y[1, r].wait_recv()
        second_norm(r)
        out_c.append(to_sibling("res", r, 1))
    pairs()
    cs = []
    for r in range(R):
        second_norm_back(r)
        cs.append(to_sibling("d2l", r, 2))
    for c in out_c:
        c.wait_recv()
    outs = [pltpu.make_async_copy(g("res"), g("res_o"), g("out_sem").at[0])]
    outs[-1].start()
    for r in range(R):
        cs[r].wait_recv()
        ffn_back(r)
        if r > 0:
            y[2, r - 1] = send_across(2, r - 1, a[2, r - 1])
        a[2, r] = send_half(2, r, ffn_back_out(r))
    y[2, R - 1] = send_across(2, R - 1, a[2, R - 1])
    ffn_weights()
    for r in range(R):
        y[2, r].wait_recv()
        first_norm_back(r)
        c = to_sibling("d1l", r, 3)
        c.wait_recv()
        attend_back(r)
        a[3, r] = send_half(3, r, attend_back_out(r))
        y[3, r] = send_across(3, r, a[3, r])
    attend_weights()
    fin = []
    for r in range(R):
        y[3, r].wait_recv()
        finish(r)
        fin.append(to_sibling("tg", r, 4))

    for k in range(7):
        g("vmine")[k : k + 1, :] = jnp.sum(g("acc")[k], axis=0, keepdims=True)
    g("vmine")[7:8, :] = jnp.zeros((1, D), F32)
    g("vmine")[7:8, 0:L] = jnp.sum(g("acc")[7], axis=0, keepdims=True)[:, :L]
    g("vmine")[7:8, 256 : 256 + L] = jnp.sum(g("acc")[8], axis=0, keepdims=True)[:, :L]
    c = remote(g("vmine"), g("vsib"), g("pool_sem").at[2], g("pool_sem").at[3], sib)
    c.start()
    c.wait()
    v = g("vmine")[...] + jnp.where(iota((8, D), 0) < 6, g("vsib")[...], 0.0)
    g("vall")[dp] = v
    vs = []
    for d in range(1, n_dp):
        t = (dp + d) % n_dp
        c = remote(g("vall").at[dp], g("vall").at[dp], g("v_s").at[d], g("v_r").at[d], (t, mp))
        c.start()
        vs.append(c)
        sends.append(c)

    if in_kernel:
        jobs = [job for j in range(3) for job in jobs_of(j)]
        depth = 6
        for wave in range(len(jobs) // 2 + depth):
            for i in range(len(jobs)):
                st = wave - i // 2
                if 0 <= st < depth:
                    jobs[i][0][st]()
        for _, end in jobs:
            end()
    else:
        gsum = grad

    for c in fin:
        c.wait_recv()
    for i, (k, o) in enumerate(((g("tg"), "tg_o"), (gsum, "g_o"), (g("loss_v"), "loss_o"))):
        outs.append(pltpu.make_async_copy(k, g(o), g("out_sem").at[1 + i]))
        outs[-1].start()
    for c in vs:
        c.wait_recv()
    v = g("vall")[0]
    for d in range(1, n_dp):
        v = v + g("vall")[d]
    g("vout")[...] = v
    outs.append(pltpu.make_async_copy(g("vout"), g("vec_o"), g("out_sem").at[4]))
    outs[-1].start()
    for c in sends:
        c.wait_send()
    for c in outs:
        c.wait()


def on_device(n_dp, tokens, lengths, send_slot, recv_place, w_query, b_query, w_key, w_value, b_value, w_out,
              output_bias, first_norm_gain, first_norm_bias, w_up, b_up, w_down, down_bias, second_norm_gain,
              second_norm_bias, out_grad):
    T, D = tokens.shape
    R, L, F = lengths.shape[0], w_query.shape[1], w_up.shape[1]
    z = sizes(n_dp, R, T, D, L, F)
    S, half, heads = z["S"], z["half"], z["heads"]
    z["in_kernel"] = n_dp == 8
    z["n_sub"] = 8
    n_jobs = 3 * z["n_sub"]
    sub = D // z["n_sub"]
    widen = lambda v: jnp.pad(v, (0, D - v.shape[0]))
    vecs = jnp.stack([
        widen(b_query), widen(b_value), output_bias, first_norm_gain, first_norm_bias, b_up, down_bias,
        second_norm_gain, second_norm_bias,
    ])
    ins = dict(lengths=lengths, send_slot=send_slot, recv_place=recv_place, vecs=vecs, tokens=tokens, wq=w_query,
               wk=w_key, wv=w_value, wo=w_out, wu=w_up, wd=w_down, og=out_grad)
    any_, vmem, smem = pl.BlockSpec(memory_space=pl.ANY), pl.BlockSpec(memory_space=pltpu.VMEM), pl.BlockSpec(memory_space=pltpu.SMEM)
    in_specs = [smem] * 3 + [vmem] + [any_] * 8
    outs = dict(
        res_o=((T, D), BF16), tg_o=((T, D), F32), g_o=((3, D, D), BF16), vec_o=((8, D), F32), loss_o=((8, 128), F32)
    )
    n_qb = S // 256
    KW = min(256 + (MAX_PIECE if n_qb <= 2 else 2 * MAX_PIECE), S)
    V = pltpu.VMEM
    dma = pltpu.SemaphoreType.DMA
    scratch = dict(
        tokens_v=V((T, D), BF16), og_v=V((T, D), BF16), wq_v=V((D, L), BF16), wk_v=V((D, L), BF16),
        wv_v=V((D, L), BF16), wo_v=V((L, D), BF16), wu_v=V((D, F), BF16), wd_v=V((F, D), BF16),
        q=V((T, L), BF16), k=V((T, L), BF16), v=V((T, L), BF16), ctx=V((T, L), BF16), dctx=V((T, L), BF16),
        dq=V((T, L), BF16), dk=V((T, L), BF16), dv=V((T, L), BF16), dk_acc=V((S, L), F32), dv_acc=V((S, L), F32),
        probs=V((R * n_qb * heads, 256, KW), BF16),
        xhat1=V((R, half, D), F32), xhat2=V((R, half, D), F32), hid=V((R, half, D), F32), d2=V((R, half, D), F32),
        d1=V((R, half, D), F32), rstd1=V((R, half, 1), F32), rstd2=V((R, half, 1), F32),
        hl=V((T, D), BF16), act=V((T, F), BF16), gp=V((T, F), BF16), d2l=V((T, D), BF16), dup=V((T, F), BF16),
        d1l=V((T, D), BF16), res=V((T, D), BF16), tg=V((T, D), F32),
        asend=V((2, R, half, D), BF16), arecv=V((2, R, half, D), BF16), own=V((R, half, D), F32),
        ysend=V((2, R, half, D), BF16), yrecv=V((2, R, half, D), BF16),
        pool=V((16, D), F32), pool_r=V((16, D), F32), dpool=V((16, D), F32), acc=V((9, 8, D), F32),
        outg=V((n_dp * 16, 128), BF16), inc=V((n_dp * 16, 128), BF16), outg2=V((n_dp * 16, 128), BF16),
        inc2=V((n_dp * 16, 128), BF16), loss_v=V((8, 128), F32),
        vmine=V((8, D), F32), vsib=V((8, D), F32), vall=V((n_dp, 8, D), F32), vout=V((8, D), F32),
        grad=V((3, D, D), BF16), gsum=V((3, D, D), BF16), rx=V((n_jobs * 3, sub // 2, D), BF16),
        rz=V((n_jobs, sub, D), BF16),
        in_sem=dma((8,)), out_sem=dma((5,)), a_s=dma((4, R)), a_r=dma((4, R)), y_s=dma((4, R)), y_r=dma((4, R)),
        g_s=dma((5, R)), g_r=dma((5, R)), pool_sem=dma((4,)), p_s=dma((2, n_dp)), p_r=dma((2, n_dp)),
        v_s=dma((n_dp,)), v_r=dma((n_dp,)), d_s=dma((n_jobs, 6)), d_r=dma((n_jobs, 6)),
    )
    names = tuple(ins) + tuple(outs) + tuple(scratch)
    res, tg, grads, vec, loss = pl.pallas_call(
        functools.partial(layer_kernel, z, names),
        out_shape=[jax.ShapeDtypeStruct(*s) for s in outs.values()],
        in_specs=in_specs,
        out_specs=[any_] * 5,
        scratch_shapes=list(scratch.values()),
        compiler_params=pltpu.CompilerParams(
            collective_id=0, has_side_effects=True, vmem_limit_bytes=63 * 2**20
        ),
    )(*ins.values())
    if not z["in_kernel"]:
        grads = lax.psum(grads, "dp")
    gd, gu, ga = grads[0].astype(F32), grads[1].astype(F32), grads[2].astype(F32)
    return (
        res, loss[0, : R * 3], tg, ga[:L].T, vec[7, :L], ga[L : 2 * L].T, ga[2 * L : 3 * L].T, vec[7, 256 : 256 + L],
        ga[3 * L :], vec[0], vec[1], vec[2], gu, vec[6], gd, vec[3], vec[4], vec[5],
    )


def solution(mesh):
    rows, flat, cut = P("dp", None), P("dp"), P("mp")
    across, down = P(None, "mp"), P("mp", None)
    return jax.shard_map(
        functools.partial(on_device, mesh.shape["dp"]),
        mesh=mesh,
        in_specs=(rows, rows, flat, flat, across, cut, across, across, cut, down, P(), P(), P(), across, cut, down,
                  P(), P(), P(), rows),
        out_specs=(rows, flat, rows, across, cut, across, across, cut, down, P(), P(), P(), across, cut, down, P(),
                   P(), P()),
        check_vma=False,
    )
```

```python
import functools
import types

import jax
import jax.numpy as jnp
from jax import lax
from jax.experimental import pallas as pl
from jax.experimental.pallas import tpu as pltpu
from jax.sharding import PartitionSpec as P

HEAD_DIM = 64
MAX_PIECE = 128
NEG_FILL = -1e30
NORM_EPS = 1e-12
UNIT_EPS = 1e-06
SIM_SCALE = 50.0
MESH = pl.DeviceIdType.MESH
F32, BF16, I32 = jnp.float32, jnp.bfloat16, jnp.int32
HIGHEST = lax.Precision.HIGHEST


def nn(a, b):
    return lax.dot_general(a, b, (((1,), (0,)), ((), ())), preferred_element_type=F32)


def nt(a, b):
    return lax.dot_general(a, b, (((1,), (1,)), ((), ())), preferred_element_type=F32)


def tn(a, b):
    return lax.dot_general(a, b, (((0,), (0,)), ((), ())), preferred_element_type=F32)


def iota(shape, axis):
    return lax.broadcasted_iota(I32, shape, axis)


def hi_lo(x):
    hi = x.astype(BF16).astype(F32)
    return hi, x - hi


def layer_kernel(z, names, *refs):
    ns = types.SimpleNamespace(**dict(zip(names, refs)))
    n_dp, R, S, D, L, F, heads = z.n_dp, z.R, z.S, z.D, z.L, z.F, z.heads
    QB, KW = z.QB, z.KW
    n_qb, half = S // QB, QB // 2
    NC = R * n_qb
    CH = D // 128
    dp, mp = lax.axis_index("dp"), lax.axis_index("mp")
    core = mp % 2
    other = 1 - core
    sib = (dp, mp + 1 - 2 * core)
    across = (dp, (mp + 2) % 4)

    bar = pltpu.get_barrier_semaphore()
    for t in (sib, across):
        pl.semaphore_signal(bar, inc=1, device_id=t, device_id_type=MESH)
    for d in range(1, n_dp):
        pl.semaphore_signal(bar, inc=1, device_id=((dp + d) % n_dp, mp), device_id_type=MESH)

    loads = []
    for i, (src, dst) in enumerate((
        (ns.tokens, ns.tokens_v), (ns.wq, ns.wq_v), (ns.wk, ns.wk_v), (ns.wv, ns.wv_v), (ns.wo, ns.wo_v),
        (ns.wu, ns.wu_v), (ns.wd, ns.wd_v), (ns.og, ns.og_v),
    )):
        loads.append(pltpu.make_async_copy(src, dst, ns.in_sem.at[i]))
        loads[-1].start()
    vecs = ns.vecs
    for i, x in enumerate((
        ns.b_query, ns.b_value, ns.output_bias, ns.first_norm_gain, ns.first_norm_bias, ns.b_up, ns.down_bias,
        ns.second_norm_gain, ns.second_norm_bias,
    )):
        n = x.shape[0]
        vecs[i : i + 1, 0:n] = x[...].reshape(1, n)
    pl.semaphore_wait(bar, 1 + n_dp)

    sends = []

    def remote(src, dst, ss, rs, to):
        return pltpu.make_async_remote_copy(
            src_ref=src, dst_ref=dst, send_sem=ss, recv_sem=rs, device_id=to, device_id_type=MESH
        )

    def vec(i, n=None):
        return vecs[i : i + 1, : (n or D)]

    ends = []
    for r in range(R):
        total, row = 0, []
        for p in range(7):
            total = total + ns.lengths[r, p]
            row.append(total)
        ends.append(row)

    def seg_of(position, r):
        seg = jnp.zeros(position.shape, I32)
        for p in range(6):
            seg = seg + jnp.where(position >= ends[r][p], 1, 0)
        return seg

    lane_head = iota((1, L), 1) // HEAD_DIM

    def only_head(x, h):
        return jnp.where(lane_head == h, x, jnp.zeros_like(x))

    in_flight = {}
    unsent = {}

    def finish_send(key):
        if key in unsent:
            sem, copy = unsent.pop(key)
            copy.wait_send()
            del in_flight[sem]

    def begin_send(key, sem, copy):
        if sem in in_flight:
            finish_send(in_flight[sem])
        in_flight[sem] = key
        unsent[key] = (sem, copy)
        copy.start()

    def pair_copy(which, c):
        par = which % 2
        return remote(ns.part.at[par, c, pl.ds(pl.multiple_of(other * half, half), half)], ns.arecv.at[par, c],
                      ns.a_s.at[par], ns.a_r.at[par, c], sib)

    def cross_copy(which, c):
        par = which % 2
        return remote(ns.ysend.at[par, c], ns.yrecv.at[par, c], ns.y_s.at[par, c], ns.y_r.at[par, c], across)

    def send_part(which, c, compute):
        part = ns.part.at[which % 2, c]

        def put(cols, val):
            part[:, cols] = val.astype(BF16)

        if which >= 2:
            finish_send((0, which - 2, c))
        compute(c, put)
        begin_send((0, which, c), (0, which % 2), pair_copy(which, c))

    def send_across(which, c):
        par = which % 2
        pair_copy(which, c).wait_recv()
        if which >= 2:
            finish_send((1, which - 2, c))
        own = pl.ds(pl.multiple_of(core * half, half), half)
        ns.ysend[par, c] = ns.part[par, c, own] + ns.arecv[par, c]
        begin_send((1, which, c), (1, which % 2, c), cross_copy(which, c))

    def y_total(which, c, rows):
        par = which % 2
        return ns.ysend[par, c, rows].astype(F32) + ns.yrecv[par, c, rows].astype(F32)

    def at_chunk(c):
        return slice(c * QB, c * QB + QB)

    def halves(i, c):
        rows = pl.ds(pl.multiple_of(c * QB + core * half, half), half)
        x = (ns.hl, ns.res, ns.d2l, ns.d1l, ns.tg)[i]
        return remote(x.at[rows], x.at[rows], ns.g_s.at[i], ns.g_r.at[G_SLOT[i], c], sib)

    def to_sibling(i, c):
        begin_send((2, i, c), (2, i), halves(i, c))

    TR = z.TR

    def by_rows(fn):
        def body(i, _):
            fn(pl.ds(pl.multiple_of(i * TR, TR), TR), i * TR)
            return 0

        lax.fori_loop(0, half // TR, body, 0, unroll=z.unroll)

    def fold(x):
        return jnp.sum(x.reshape(x.shape[0] // 8, 8, x.shape[1]), axis=0)

    def row_ds(c, start, n):
        return pl.ds(pl.multiple_of(c * QB + core * half + start, n), n)

    def columns(width, step=256):
        return [slice(n, n + step) for n in range(0, width, step)]

    def project(r):
        rows = pl.ds(r * S, S)
        x = ns.tokens_v[rows, :]
        ns.q[rows, :] = ((nt(x, ns.wq_v[...]) + vec(0, L)).astype(BF16) * (HEAD_DIM**-0.5)).astype(BF16)
        ns.k[rows, :] = nt(x, ns.wk_v[...]).astype(BF16)
        ns.v[rows, :] = (nt(x, ns.wv_v[...]) + vec(1, L)).astype(BF16)

    def win(b):
        return min(max(b * QB - MAX_PIECE, 0), S - KW)

    def attend(c):
        r, b = c // n_qb, c % n_qb
        q0, k0 = c * QB, r * S + win(b)
        same = seg_of(iota((QB, 1), 0) + b * QB, r) == seg_of(iota((1, KW), 1) + win(b), r)
        qb = ns.q[q0 : q0 + QB, :]
        kb = ns.k[k0 : k0 + KW, :]
        vb = ns.v[k0 : k0 + KW, :]
        ctx = None
        for h in range(heads):
            s = jnp.where(same, nt(only_head(qb, h), kb), NEG_FILL)
            e = jnp.exp(s - jnp.max(s, axis=-1, keepdims=True))
            p = (e * (1.0 / jnp.sum(e, axis=-1, keepdims=True))).astype(BF16)
            ns.probs[c * heads + h] = p
            o = nn(p, only_head(vb, h))
            ctx = o if ctx is None else ctx + o
        ns.ctx[q0 : q0 + QB, :] = ctx.astype(BF16)

    def attn_out(c, put):
        x = ns.ctx[at_chunk(c), :]
        for w in columns(D):
            put(w, nn(x, ns.wo_v[:, w]))

    def norm(v):
        mean = jnp.mean(v, axis=-1, keepdims=True)
        d = v - mean
        rstd = lax.rsqrt(jnp.mean(d * d, axis=-1, keepdims=True) + NORM_EPS)
        return d * rstd, rstd

    def first_norm(c):
        def body(rows, start):
            mine = row_ds(c, start, TR)
            xh, rstd = norm(ns.tokens_v[mine].astype(F32) + y_total(0, c, rows) + vec(2))
            ns.xhat1[c, rows] = xh
            ns.rstd1[c, rows] = rstd
            h = xh * vec(3) + vec(4)
            ns.hid[c, rows] = h
            ns.hl[mine] = h.astype(BF16)

        by_rows(body)

    def ffn_up(c):
        x = ns.hl[at_chunk(c), :]
        for w in columns(F):
            u = nn(x, ns.wu_v[:, w]) + vecs[5:6, w]
            phi = 0.5 + 0.5 * lax.erf(u * 0.7071067811865476)
            ns.act[at_chunk(c), w] = (u * phi).astype(BF16)
            ns.gp[at_chunk(c), w] = (phi + u * (jnp.exp(-0.5 * (u * u)) * 0.3989422804014327)).astype(BF16)

    def ffn_down(c, put):
        x = ns.act[at_chunk(c), :]
        for w in columns(D):
            put(w, nn(x, ns.wd_v[:, w]))

    def second_norm(c):
        r, b = c // n_qb, c % n_qb

        def body(rows, start):
            xh, rstd = norm(ns.hid[c, rows] + y_total(1, c, rows) + vec(6))
            ns.xhat2[c, rows] = xh
            ns.rstd2[c, rows] = rstd
            res = xh * vec(7) + vec(8)
            low = res.astype(BF16)
            ns.res[row_ds(c, start, TR)] = low
            ns.rest[rows] = (res - low.astype(F32)).astype(BF16)

        by_rows(body)
        piece = iota((8, half), 0)
        seg = seg_of(iota((8, half), 1) + (core * half + b * QB), r)
        member = jnp.where((seg == piece) & (piece < 6), 1.0, 0.0).astype(BF16)
        at = slice(r * 8, r * 8 + 8)
        ns.pool[at, :] += nn(member, ns.res[row_ds(c, 0, half)]) + nn(member, ns.rest[...])

    PR = 16
    n_sent = R * 6

    def per_row(values, axis, shape, fill):
        pos = iota(shape, axis) % PR
        out = jnp.full(shape, fill, I32)
        for s in range(n_sent):
            out = jnp.where(pos == (s // 6) * 8 + s % 6, values[s], out)
        return out

    def slot_onehot(axis):
        shape = (n_dp * 16, CH * PR) if axis == 1 else (CH * PR, n_dp * 16)
        line = (1, CH * PR) if axis == 1 else (CH * PR, 1)
        vals = [ns.send_slot[s] // 2 * 16 + ns.send_slot[s] % 2 for s in range(n_sent)]
        target = per_row(vals, axis if axis == 1 else 0, line, -65536) + iota(line, 1 if axis == 1 else 0) // PR * 2
        return jnp.where(iota(shape, 0 if axis == 1 else 1) == target, 1.0, 0.0).astype(BF16)

    def place_onehot(axis):
        line = (1, n_dp * 16) if axis == 1 else (n_dp * 16, 1)
        shape = (CH * PR, n_dp * 16) if axis == 1 else (n_dp * 16, CH * PR)
        pos = iota(line, axis)
        slot = pos // 16 * 2 + pos % 2
        target = jnp.zeros(line, I32)
        for s in range(2 * n_dp):
            target = jnp.where(slot == s, ns.recv_place[s], target)
        target = target + pos % 16 // 2 * PR
        return jnp.where(iota(shape, 0 if axis == 1 else 1) == target, 1.0, 0.0).astype(BF16)

    def stack(x):
        return jnp.concatenate([x[:, c * 128 : c * 128 + 128] for c in range(CH)], axis=0)

    def unstack(x):
        return jnp.concatenate([x[c * PR : c * PR + PR] for c in range(CH)], axis=1)

    def peers(src, dst, ssem, rsem):
        cs = []
        mine = pl.ds(pl.multiple_of(dp * 16, 16), 16)
        for d in range(1, n_dp):
            t = (dp + d) % n_dp
            c = remote(src.at[pl.ds(pl.multiple_of(t * 16, 16), 16)], dst.at[mine], ssem.at[d], rsem.at[d], (t, mp))
            c.start()
            cs.append(c)
        dst[mine] = src[mine]
        for c in cs:
            c.wait()

    def pairs():
        c = remote(ns.pool, ns.pool_r, ns.pool_sem.at[0], ns.pool_sem.at[1], sib)
        c.start()
        lens = [ns.lengths[s // 6, s % 6] for s in range(n_sent)]
        size = per_row(lens, 0, (PR, 1), 1).astype(F32)
        inv = 1.0 / size
        hot = slot_onehot(1)
        c.wait()
        pooled = (ns.pool[...] + ns.pool_r[...]) * inv
        ns.outg[...] = nn(hot, stack(pooled).astype(BF16)).astype(BF16)
        peers(ns.outg, ns.inc, ns.p_s, ns.p_r.at[0])
        o = unstack(nn(place_onehot(1), ns.inc[...]))
        s = lax.rsqrt(jnp.sum(o * o, axis=-1, keepdims=True) + UNIT_EPS)
        u = o * s
        logits = SIM_SCALE * lax.dot_general(
            u, u, (((1,), (1,)), ((), ())), precision=HIGHEST, preferred_element_type=F32
        )
        i, j = iota((PR, PR), 0), iota((PR, PR), 1)
        live = (i % 2 == 0) & (i < n_sent) & (j % 2 == 1) & (j < n_sent)
        lm = jnp.where(live, logits, NEG_FILL)
        peak = jnp.max(lm, axis=-1, keepdims=True)
        e = jnp.where(live, jnp.exp(lm - peak), 0.0)
        tot = jnp.maximum(jnp.sum(e, axis=-1, keepdims=True), 1e-30)
        partner = live & (j == i + 1)
        loss = peak + jnp.log(tot) - jnp.sum(jnp.where(partner, logits, 0.0), axis=-1, keepdims=True)
        i2, j2 = iota((PR, 128), 0), iota((PR, 128), 1)
        ns.loss_v[...] = jnp.broadcast_to(
            jnp.sum(jnp.where((i2 == 2 * j2) & (i2 < n_sent), loss, 0.0), axis=0, keepdims=True), (8, 128)
        )
        dl = e / tot - jnp.where(partner, 1.0, 0.0)
        du = SIM_SCALE * (
            lax.dot_general(dl, u, (((1,), (0,)), ((), ())), precision=HIGHEST, preferred_element_type=F32)
            + lax.dot_general(dl, u, (((0,), (0,)), ((), ())), precision=HIGHEST, preferred_element_type=F32)
        )
        do = s * (du - u * jnp.sum(u * du, axis=-1, keepdims=True))
        ns.outg2[...] = nn(place_onehot(0), stack(do).astype(BF16)).astype(BF16)
        peers(ns.outg2, ns.inc2, ns.p_s, ns.p_r.at[1])
        ns.dpool[...] = unstack(nn(slot_onehot(0), ns.inc2[...])) * inv

    def norm_back(dx, xh, rstd):
        return rstd * (
            dx - jnp.mean(dx, axis=-1, keepdims=True) - xh * jnp.mean(dx * xh, axis=-1, keepdims=True)
        )

    def second_norm_back(c):
        r, b = c // n_qb, c % n_qb
        hi, lo = hi_lo(ns.dpool[r * 8 : r * 8 + 8, :])
        lane = iota((half, 16), 1) % 8
        seg = seg_of(iota((half, 1), 0) + (core * half + b * QB), r)
        member = jnp.where((seg == lane) & (lane < 6), 1.0, 0.0).astype(BF16)
        ns.dtok[...] = nn(member, jnp.concatenate([hi, lo], axis=0).astype(BF16))

        def body(rows, start):
            mine = row_ds(c, start, TR)
            d = ns.og_v[mine].astype(F32) + ns.dtok[rows]
            xh = ns.xhat2[c, rows]
            ns.acc[4] += fold(d * xh)
            ns.acc[5] += fold(d)
            d2 = norm_back(d * vec(7), xh, ns.rstd2[c, rows])
            ns.acc[3] += fold(d2)
            ns.d2[c, rows] = d2
            ns.d2l[mine] = d2.astype(BF16)

        by_rows(body)

    def ffn_back(c):
        rows = at_chunk(c)
        x = ns.d2l[rows, :]
        for w in columns(F):
            da = nt(x, ns.wd_v[w, :]).astype(BF16)
            du = (da.astype(F32) * ns.gp[rows, w].astype(F32)).astype(BF16)
            ns.dup[rows, w] = du
            ns.acc[6, :, w] += fold(du.astype(F32))

    def ffn_back_out(c, put):
        x = ns.dup[at_chunk(c), :]
        for w in columns(D):
            put(w, nt(x, ns.wu_v[w, :]))

    def down_weights(n):
        for w in columns(F)[n : n + 1]:
            grad[0, w, :] = tn(ns.act[:, w], ns.d2l[...]).astype(BF16)

    def up_weights(n):
        for w in columns(D)[n : n + 1]:
            grad[1, w, :] = tn(ns.hl[:, w], ns.dup[...]).astype(BF16)

    def first_norm_back(c):
        def body(rows, start):
            mine = row_ds(c, start, TR)
            d = ns.d2[c, rows] + y_total(2, c, rows)
            xh = ns.xhat1[c, rows]
            ns.acc[1] += fold(d * xh)
            ns.acc[2] += fold(d)
            d1 = norm_back(d * vec(3), xh, ns.rstd1[c, rows])
            ns.acc[0] += fold(d1)
            ns.d1[c, rows] = d1
            ns.d1l[mine] = d1.astype(BF16)

        by_rows(body)

    def attend_back(c):
        r, b = c // n_qb, c % n_qb
        q0, k0 = c * QB, r * S + win(b)
        cb = nt(ns.d1l[at_chunk(c), :], ns.wo_v[...]).astype(BF16)
        qb = ns.q[q0 : q0 + QB, :]
        kb = ns.k[k0 : k0 + KW, :]
        vb = ns.v[k0 : k0 + KW, :]
        dq = dk = dv = None
        for h in range(heads):
            p = ns.probs[c * heads + h]
            dp_ = nt(cb, only_head(vb, h))
            pf = p.astype(F32)
            delta = jnp.sum(pf * dp_, axis=-1, keepdims=True)
            ds = (pf * (dp_ - delta)).astype(BF16)
            t, u, w = nn(ds, only_head(kb, h)), tn(ds, only_head(qb, h)), tn(p, only_head(cb, h))
            dq, dk, dv = (t, u, w) if dq is None else (dq + t, dk + u, dv + w)
        dq = (dq * (HEAD_DIM**-0.5)).astype(BF16)
        ns.dq[q0 : q0 + QB, :] = dq
        ns.acc[7, :, :L] += fold(dq.astype(F32))
        at = slice(win(b), win(b) + KW)
        if b == 0:
            ns.dk_acc[...] = jnp.zeros((S, L), F32)
            ns.dv_acc[...] = jnp.zeros((S, L), F32)
        ns.dk_acc[at, :] += dk
        ns.dv_acc[at, :] += dv
        if b == n_qb - 1:
            rows = slice(r * S, r * S + S)
            ns.dk[rows, :] = ns.dk_acc[...].astype(BF16)
            dvr = ns.dv_acc[...].astype(BF16)
            ns.dv[rows, :] = dvr
            ns.acc[8, :, :L] += fold(dvr.astype(F32))

    def attend_back_out(c, put):
        at = at_chunk(c)
        for w in columns(D):
            put(
                w,
                nn(ns.dq[at, :], ns.wq_v[:, w])
                + nn(ns.dk[at, :], ns.wk_v[:, w])
                + nn(ns.dv[at, :], ns.wv_v[:, w]),
            )

    def attend_weights():
        for i, x in enumerate((ns.dq, ns.dk, ns.dv)):
            grad[2, i * L : i * L + L, :] = tn(x[...], ns.tokens_v[...]).astype(BF16)
        grad[2, 3 * L : 4 * L, :] = tn(ns.ctx[...], ns.d1l[...]).astype(BF16)

    def finish(c):
        def body(rows, start):
            ns.tg[row_ds(c, start, TR)] = ns.d1[c, rows] + y_total(3, c, rows)

        by_rows(body)

    xi, zi = dp % 2, dp // 2
    nz = n_dp // 2
    in_kernel = z.in_kernel
    outer = (zi == 0) | (zi == nz - 1)
    inner = (zi != 0) & (zi != nz - 1)
    xp = (dp + 1 - 2 * xi, mp)
    zp = (dp + 2 - 4 * (zi % 2), mp)
    zq = ((dp + 2 * (3 - 2 * zi)) % n_dp if in_kernel else dp, mp)
    ii = zi // 2
    grad, gsum = ns.grad, ns.gsum

    def when(condition, fn):
        return lambda: pl.when(condition)(fn)

    def add_into(dst, dst_at, a_at, b_at, n):
        step = 48 if n % 48 == 0 else 32 if n % 32 == 0 else 16

        def body(i, _):
            o = i * step
            x = grad[a_at[0], pl.ds(pl.multiple_of(a_at[1] + o, 16), step), :]
            y = ns.rx[pl.ds(pl.multiple_of(b_at + o, 16), step), :]
            dst[dst_at[0], pl.ds(pl.multiple_of(dst_at[1] + o, 16), step), :] = x + y
            return 0

        lax.fori_loop(0, n // step, body, 0)

    def x_job(slot, j, r0, n):
        h = n // 2
        mine = pl.multiple_of(r0 + xi * h, 16)
        yours = pl.multiple_of(r0 + (1 - xi) * h, 16)
        own, theirs = pl.ds(mine, h), pl.ds(yours, h)
        s = lambda k: ns.d_s.at[z.slots[slot], k]
        q = lambda k: ns.d_r.at[slot, k]
        b0 = z.rx_at[slot]
        buf = lambda k: ns.rx.at[pl.ds(b0 + k * h, h)]
        x1 = remote(grad.at[j, theirs], buf(0), s(0), q(0), xp)
        z1 = remote(grad.at[j, own], buf(1), s(0), q(1), zp)
        z2 = remote(grad.at[j, own], buf(2), s(0), q(2), zq)
        z3 = remote(gsum.at[j, own], gsum.at[j, own], s(1), q(1), zp)
        x2 = remote(gsum.at[j, own], gsum.at[j, own], s(0), q(3), xp)

        def s1o():
            x1.wait()
            add_into(grad, (j, mine), (j, mine), b0, h)
            z1.start()

        def s1i():
            x1.wait()
            add_into(grad, (j, mine), (j, mine), b0, h)

        def s2():
            z1.wait_recv()
            add_into(grad, (j, mine), (j, mine), b0 + h, h)
            z2.start()

        def s3():
            z2.wait()
            add_into(gsum, (j, mine), (j, mine), b0 + 2 * h, h)
            z3.start()
            x2.start()

        def s4():
            z3.wait_recv()
            z1.wait_send()
            x2.start()

        def end():
            x2.wait_send()
            pl.when(inner)(z3.wait_send)

        steps = {0: x1.start, 1: when(outer, s1o), 8: when(inner, s1i), 2: when(inner, s2), 3: when(inner, s3),
                 4: when(outer, s4), 5: x2.wait_recv}
        return steps, end

    def z_job(slot, j, r0, n):
        h = n // 2
        mine = pl.multiple_of(r0 + ii * h, 16)
        yours = pl.multiple_of(r0 + (1 - ii) * h, 16)
        own, theirs, whole = pl.ds(mine, h), pl.ds(yours, h), pl.ds(r0, n)
        s = lambda k: ns.d_s.at[z.slots[slot], k]
        q = lambda k: ns.d_r.at[slot, k]
        b0 = z.rx_at[slot]
        buf = lambda k: ns.rx.at[pl.ds(b0 + k * h, h)]
        z1 = remote(grad.at[j, whole], ns.rx.at[pl.ds(b0 + n, n)], s(0), q(0), zp)
        z2 = remote(grad.at[j, theirs], buf(0), s(0), q(1), zq)
        x = remote(grad.at[j, own], buf(1), s(1), q(2), xp)
        z2b = remote(gsum.at[j, own], gsum.at[j, own], s(0), q(3), zq)
        z3a = remote(gsum.at[j, own], gsum.at[j, own], s(1), q(1), zp)
        z3b = remote(gsum.at[j, theirs], gsum.at[j, theirs], s(0), q(2), zp)

        def s1():
            z1.wait_recv()
            add_into(grad, (j, r0), (j, r0), b0 + n, n)
            z2.start()

        def s2():
            z2.wait_recv()
            add_into(grad, (j, mine), (j, mine), b0, h)
            x.start()

        def s3():
            x.wait()
            z2.wait_send()
            add_into(gsum, (j, mine), (j, mine), b0 + h, h)
            z2b.start()
            z3a.start()

        def s4():
            z2b.wait()
            z3b.start()

        def s5():
            z3a.wait_recv()
            z3b.wait_recv()

        def end():
            pl.when(outer)(z1.wait_send)

            @pl.when(inner)
            def _():
                z3a.wait_send()
                z3b.wait_send()

        steps = {0: when(outer, z1.start), 1: when(inner, s1), 2: when(inner, s2), 3: when(inner, s3),
                 4: when(inner, s4), 5: when(outer, s5)}
        return steps, end

    def q_job(slot, j, r0, n):
        h, f = n // 2, n // 4
        mine = pl.multiple_of(r0 + ii * h, 16)
        yours = pl.multiple_of(r0 + (1 - ii) * h, 16)
        own, theirs, whole = pl.ds(mine, h), pl.ds(yours, h), pl.ds(r0, n)
        back_a = pl.ds(pl.multiple_of(mine + xi * f, 16), f)
        back_b = pl.ds(pl.multiple_of(yours + xi * f, 16), f)
        s = lambda k: ns.d_s.at[z.slots[slot], k]
        q = lambda k: ns.d_r.at[slot, k]
        b0 = z.rx_at[slot]
        buf = lambda k: ns.rx.at[pl.ds(b0 + k * h, h)]
        z1 = remote(grad.at[j, whole], ns.rx.at[pl.ds(b0 + n, n)], s(0), q(0), zp)
        z2 = remote(grad.at[j, theirs], buf(0), s(0), q(1), zq)
        x = remote(grad.at[j, own], buf(1), s(1), q(2), xp)
        z2b = remote(gsum.at[j, own], gsum.at[j, own], s(0), q(3), zq)
        z3a = remote(gsum.at[j, back_a], gsum.at[j, back_a], s(1), q(0), zp)
        z3b = remote(gsum.at[j, back_b], gsum.at[j, back_b], s(0), q(1), zp)
        xa = remote(gsum.at[j, back_a], gsum.at[j, back_a], s(0), q(2), xp)
        xb = remote(gsum.at[j, back_b], gsum.at[j, back_b], s(1), q(3), xp)

        def s1():
            z1.wait_recv()
            add_into(grad, (j, r0), (j, r0), b0 + n, n)
            z2.start()

        def s2():
            z2.wait_recv()
            add_into(grad, (j, mine), (j, mine), b0, h)
            x.start()

        def s3():
            x.wait()
            z2.wait_send()
            add_into(gsum, (j, mine), (j, mine), b0 + h, h)
            z2b.start()
            z3a.start()

        def s4():
            z2b.wait()
            z3b.start()

        def s5():
            z3a.wait_recv()
            z1.wait_send()
            xa.start()
            z3b.wait_recv()
            xb.start()

        def s6():
            xa.wait_recv()
            xb.wait_recv()

        def end():
            @pl.when(outer)
            def _():
                xa.wait_send()
                xb.wait_send()

            @pl.when(inner)
            def _():
                z3a.wait_send()
                z3b.wait_send()

        steps = {0: when(outer, z1.start), 1: when(inner, s1), 2: when(inner, s2), 3: when(inner, s3),
                 4: when(inner, s4), 5: when(outer, s5), 6: when(outer, s6)}
        return steps, end

    def u_job(slot, j, r0, n):
        near = pl.multiple_of(r0 + ii * n, 16)
        far = pl.multiple_of(r0 + (1 - ii) * n, 16)
        near_d, far_d = pl.ds(near, n), pl.ds(far, n)
        s = lambda k: ns.d_s.at[z.slots[slot], k]
        q = lambda k: ns.d_r.at[slot, k]
        b0 = z.rx_at[slot]
        buf = lambda k: ns.rx.at[pl.ds(b0 + k * n, n)]
        za = remote(grad.at[j, far_d], buf(0), s(0), q(0), zp)
        ma = remote(grad.at[j, far_d], buf(1), s(0), q(1), zq)
        zb = remote(grad.at[j, near_d], buf(0), s(1), q(0), zp)
        xa = remote(grad.at[j, near_d], buf(1), s(1), q(1), xp)
        zc = remote(gsum.at[j, near_d], gsum.at[j, near_d], s(0), q(2), zp)
        mb = remote(gsum.at[j, near_d], gsum.at[j, near_d], s(0), q(3), zq)
        zd = remote(gsum.at[j, far_d], gsum.at[j, far_d], s(1), q(2), zp)

        def s1():
            za.wait_recv()
            add_into(grad, (j, far), (j, far), b0, n)
            ma.start()

        def s2():
            ma.wait_recv()
            add_into(grad, (j, near), (j, near), b0 + n, n)
            zb.start()

        def s3():
            zb.wait_recv()
            add_into(grad, (j, near), (j, near), b0, n)
            xa.start()

        def s4():
            xa.wait_recv()
            za.wait_send()
            add_into(gsum, (j, near), (j, near), b0 + n, n)
            zc.start()

        def s5():
            zc.wait_recv()
            ma.wait_send()
            mb.start()

        def s6():
            mb.wait_recv()
            zb.wait_send()
            zd.start()

        def end():
            @pl.when(outer)
            def _():
                xa.wait_send()
                zc.wait_send()

            @pl.when(inner)
            def _():
                mb.wait_send()
                zd.wait_send()

        steps = {0: when(outer, za.start), 1: when(inner, s1), 2: when(inner, s2), 3: when(outer, s3),
                 4: when(outer, s4), 5: when(inner, s5), 6: when(inner, s6), 7: when(outer, zd.wait_recv)}
        return steps, end

    def vector_job():
        vg, vr = ns.vg, ns.vr
        s = lambda k: ns.v_s.at[k]
        q = lambda k: ns.v_r.at[k]
        z1 = remote(vg, vr.at[0], s(0), q(0), zp)
        z2 = remote(vg, vr.at[1], s(0), q(1), zq)
        x = remote(vg, vr.at[2], s(1), q(2), xp)
        z3 = remote(ns.vt, ns.vt, s(0), q(0), zp)

        def c1():
            z1.wait_recv()
            vg[...] = vg[...] + vr[0]
            z2.start()

        def c2():
            z2.wait_recv()
            z2.wait_send()
            vg[...] = vg[...] + vr[1]
            x.start()

        def c3():
            x.wait_recv()
            ns.vt[...] = vg[...] + vr[2]
            z3.start()

        def end():
            pl.when(outer)(z1.wait_send)

            @pl.when(inner)
            def _():
                x.wait_send()
                z3.wait_send()

        steps = {0: when(outer, z1.start), 1: when(inner, c1), 2: when(inner, c2), 3: when(inner, c3),
                 4: when(outer, z3.wait_recv)}
        return steps, end

    tasks, ends_of = {}, {}
    if in_kernel:
        for i, (kind, j, r0, n) in enumerate(z.jobs):
            steps, end = (x_job, z_job, q_job, u_job)[kind](i, j, r0, n)
            tasks.update({JOB + i * 10 + k: f for k, f in steps.items()})
            ends_of[i] = end
        steps, end = vector_job()
        tasks.update({VECTOR + k: f for k, f in steps.items()})
        ends_of[-1] = end

    waited = set()

    def once(key, fn):
        if key not in waited:
            waited.add(key)
            fn()

    def load(*keys):
        for k in keys:
            once((9, k), loads[k].wait)

    def come(i, c):
        once((i, c), halves(i, c).wait_recv)

    ns.pool[...] = jnp.zeros((PR, D), F32)
    ns.acc[...] = jnp.zeros(ns.acc.shape, F32)

    def run_project(r):
        load(0, 1, 2, 3)
        project(r)

    def run_out(c):
        load(4)
        send_part(0, c, attn_out)

    def run_norm(c):
        cross_copy(0, c).wait_recv()
        first_norm(c)
        to_sibling(0, c)

    def run_up(c):
        load(5)
        come(0, c)
        ffn_up(c)

    def run_down(c):
        load(6)
        send_part(1, c, ffn_down)

    def run_second(c):
        cross_copy(1, c).wait_recv()
        second_norm(c)
        to_sibling(1, c)

    forward = (run_project, attend, run_out, functools.partial(send_across, 0), run_norm, run_up, run_down,
               functools.partial(send_across, 1), run_second)
    if NC == 4:
        plan = FORWARD
    else:
        plan = [r for r in range(R)]
        for group in ((1, 2, 3), (4, 5, 6, 7), (8,)):
            plan += [10 * k + c for c in range(NC) for k in group]
    for k in plan:
        forward[k // 10](k % 10)
    load(7)
    pairs()

    def run_second_back(c):
        second_norm_back(c)
        to_sibling(2, c)

    def run_down_weights(n):
        for i in range(NC):
            come(2, i)
        down_weights(n)

    def run_ffn_back(c):
        come(2, c)
        ffn_back(c)

    def run_first_back(c):
        cross_copy(2, c).wait_recv()
        first_norm_back(c)
        to_sibling(3, c)

    def run_attend_back(c):
        come(3, c)
        attend_back(c)

    def run_finish(c):
        cross_copy(3, c).wait_recv()
        finish(c)
        to_sibling(4, c)

    def run_results(_):
        for i in range(NC):
            come(1, i)

    def vector_copy():
        return remote(ns.vmine, ns.vsib, ns.pool_sem.at[2], ns.pool_sem.at[3], sib)

    def run_vectors(_):
        for i in range(7):
            ns.vmine[i : i + 1, :] = jnp.sum(ns.acc[i], axis=0, keepdims=True)
        ns.vmine[7:8, :] = jnp.zeros((1, D), F32)
        ns.vmine[7:8, 0:L] = jnp.sum(ns.acc[7], axis=0, keepdims=True)[:, :L]
        ns.vmine[7:8, 256 : 256 + L] = jnp.sum(ns.acc[8], axis=0, keepdims=True)[:, :L]
        vector_copy().start()

    def run_vectors_sum(_):
        vector_copy().wait()
        v = ns.vmine[...] + jnp.where(iota((8, D), 0) < 6, ns.vsib[...], 0.0)
        ns.vg[...] = jnp.concatenate([v[:, : D // 2], v[:, D // 2 :]], axis=0).astype(BF16)

    backward = (
        run_second_back, run_down_weights, run_ffn_back, lambda c: send_part(2, c, ffn_back_out),
        functools.partial(send_across, 2), up_weights, run_first_back, run_attend_back,
        lambda c: send_part(3, c, attend_back_out), functools.partial(send_across, 3), lambda _: attend_weights(),
        run_finish, functools.partial(come, 4), run_results, run_vectors, run_vectors_sum,
    )
    for k in z.order:
        if k in tasks:
            if k in z.free_before:
                ends_of.pop(z.free_before[k])()
            tasks[k]()
        elif k < VECTOR:
            backward[k // 10](k % 10)
    for end in ends_of.values():
        end()
    if not in_kernel:
        gsum[...] = grad[...]
        ns.vt[...] = ns.vg[...]
    for key in list(unsent):
        finish_send(key)
    for c in sends:
        c.wait_send()


def unpack_kernel(z, g, res_i, tg_i, vec, loss_i, gd, gu, res, tg, gq, gk, gv, go, *more):
    L, R, D = z.L, z.R, z.D
    ones, (bq, bv, loss, wide, sem) = more[:7], more[7:]
    stores = []

    def store(src, dst):
        stores.append(pltpu.make_async_copy(src, dst, sem.at[len(stores)]))
        stores[-1].start()

    rows = tg.shape[0] // 4
    for i in range(4):
        at = pl.ds(i * rows, rows)
        store(tg_i.at[at], tg.at[at])
    for m in range(3):
        for i, r in enumerate(range(0, D, L)):
            at = pl.ds(r, L)
            wide[m, at] = g[m, at].astype(F32)
            store(wide.at[m, at], (gq, gk, gv, go)[i] if m == 2 else (gd, gu)[m].at[at])
    for i in range(2):
        at = pl.ds(2 * i * rows, 2 * rows)
        store(res_i.at[at], res.at[at])
    v = vec[...].astype(F32)
    v = jnp.concatenate([v[:8], v[8:]], axis=1)
    for n, one in enumerate(ones):
        one[...] = v[n, :]
    bq[...] = v[7, 0:L]
    bv[...] = v[7, 256 : 256 + L]
    loss[...] = loss_i[0, 0 : R * 3]
    for c in stores:
        c.wait()


FORWARD = (
    0, 10, 20, 1, 30, 11, 21, 12, 31, 22, 13, 32, 23, 33, 40, 50, 60, 41, 70, 51, 61, 42, 71, 52, 62, 43, 72,
    53, 63, 73, 80, 81, 82, 83,
)
JOBS = (
    (0, 0, 32), (1, 0, 32), (3, 0, 80), (0, 0, 32), (0, 0, 96), (1, 0, 64), (0, 0, 96), (0, 0, 96), (1, 0, 64),
    (0, 0, 96), (3, 1, 80), (0, 1, 96), (1, 1, 96), (0, 1, 96), (0, 1, 96), (0, 1, 96), (1, 1, 64), (0, 1, 64),
    (0, 2, 96), (1, 2, 64), (0, 2, 96), (1, 2, 64), (0, 2, 96), (1, 2, 64), (0, 2, 96), (1, 2, 64), (0, 2, 64),
    (1, 2, 64),
)
VECTOR, JOB = 200, 1000
ORDER = (
    0, 1, 2, 3, 21, 10, 1010, 1000, 11, 1040, 1030, 1020, 12, 1070, 22, 1050, 31, 23, 20, 1080, 1060, 30, 1048,
    1011, 50, 51, 1110, 1021, 41, 1012, 1100, 1051, 40, 1013, 1130, 32, 1078, 1120, 52, 1081, 1068, 1041, 1071,
    42, 1052, 1022, 61, 1101, 1170, 1160, 1140, 1001, 33, 1053, 1121, 1082, 1061, 1178, 1014, 1141, 1150, 60,
    1102, 1042, 43, 1031, 70, 1072, 1090, 1138, 1054, 71, 1122, 1023, 1083, 1161, 1148, 1008, 1043, 1073, 1131,
    1062, 62, 1151, 1002, 1103, 80, 1091, 63, 1142, 1098, 1158, 1123, 1084, 72, 1162, 1132, 1063, 1118, 1024,
    73, 140, 1003, 90, 1143, 1152, 100, 82, 1190, 1104, 1092, 1111, 1124, 1163, 81, 1133, 150, 92, 1180, 1210,
    1220, 1025, 1240, 1004, 1074, 1144, 1191, 91, 1250, 1153, 83, 1093, 1015, 1038, 1105, 1055, 1026, 1164,
    130, 1171, 1145, 1032, 1260, 1211, 93, 1192, 200, 1112, 1154, 1181, 1064, 1200, 1106, 1075, 1033, 1230,
    1188, 1228, 110, 1270, 1085, 1251, 1134, 201, 1172, 1212, 1193, 1221, 1034, 1113, 1261, 120, 1044, 1182,
    1231, 112, 1201, 1173, 1213, 1174, 111, 1114, 1252, 1005, 1094, 121, 1271, 1194, 202, 1248, 1107, 1183,
    1268, 1035, 1241, 1222, 1184, 1095, 1224, 204, 1065, 1214, 1027, 1215, 1232, 1125, 1253, 1208, 1202, 203,
    1135, 1204, 113, 1272, 1264, 1262, 1244, 1223, 1185, 1242, 1233, 1155, 1115, 1175, 1255, 1203, 1045, 1263,
    123, 122, 1243, 1225, 1165, 1205, 1273, 1265, 1195, 1254, 1245, 1234, 1235, 1274, 1275,
)
G_SLOT = (0, 1, 0, 0, 2)
VMEM1 = 54 * 2**20


def send_slots(order, n_jobs):
    steps = [(n, k, (k - JOB) // 10) for n, k in enumerate(order) if k >= JOB]
    last = {i: n for n, _, i in steps}
    slots, free_before, done, used = {}, {}, [], 0
    for n, k, i in steps:
        if i not in slots:
            if done:
                old = done.pop(0)
                slots[i], free_before[k] = slots[old], old
            else:
                slots[i], used = used, used + 1
        if last[i] == n:
            done.append(i)
    return slots, free_before, used


def default_order(chunks):
    out = []
    for group in ((0,), (2, 3, 4)):
        out += [10 * k + c for c in range(chunks) for k in group]
    out += [130, 10, 11, 12, 50, 51, 52]
    for group in ((6,), (7,), (8, 9), (11, 12)):
        out += [10 * k + c for c in range(chunks) for k in group]
    return out + [100, 140, 150]


def on_device(n_dp, tokens, lengths, send_slot, recv_place, w_query, b_query, w_key, w_value, b_value, w_out,
              output_bias, first_norm_gain, first_norm_bias, w_up, b_up, w_down, down_bias, second_norm_gain,
              second_norm_bias, out_grad):
    T, D = tokens.shape
    R, L, F = lengths.shape[0], w_query.shape[1], w_up.shape[1]
    S, heads = T // R, L // HEAD_DIM
    QB = 256 if S % 256 == 0 else S
    n_qb, half = S // QB, QB // 2
    KW = min(QB + (MAX_PIECE if n_qb <= 2 else 2 * MAX_PIECE), S)
    NC = R * n_qb
    jobs, rx_at, rx_rows, at = [], [], 0, [0, 0, 0]
    for kind, j, n in JOBS:
        jobs.append((kind, j, at[j], n))
        rx_at.append(rx_rows)
        at[j] += 2 * n if kind == 3 else n
        rx_rows += n // 2 * 3 if kind == 0 else 2 * n
    n_jobs = len(jobs)
    slots, free_before, n_slots = send_slots(ORDER, n_jobs)
    order = ORDER if NC == 4 else default_order(NC)
    in_kernel = n_dp == 8 and at == [D, D, D] and NC == 4
    z = types.SimpleNamespace(n_dp=n_dp, R=R, S=S, D=D, L=L, F=F, heads=heads, in_kernel=in_kernel, QB=QB, KW=KW, TR=32,
                              unroll=4, jobs=jobs, rx_at=rx_at, order=order, slots=slots, free_before=free_before)
    ins = dict(lengths=lengths, send_slot=send_slot, recv_place=recv_place, b_query=b_query, b_value=b_value,
               output_bias=output_bias, first_norm_gain=first_norm_gain, first_norm_bias=first_norm_bias, b_up=b_up,
               down_bias=down_bias, second_norm_gain=second_norm_gain, second_norm_bias=second_norm_bias,
               tokens=tokens, wq=w_query.T, wk=w_key.T, wv=w_value.T, wo=w_out, wu=w_up, wd=w_down, og=out_grad)
    any_, vmem, smem = (pl.BlockSpec(memory_space=m) for m in (pl.ANY, pltpu.VMEM, pltpu.SMEM))
    in_specs = [smem] * 3 + [vmem] * 9 + [any_] * 8
    outs = dict(
        res=((T, D), BF16), tg=((T, D), F32), gsum=((3, D, D), BF16), vt=((16, D // 2), BF16), loss_v=((8, 128), F32)
    )
    V = pltpu.VMEM
    dma = pltpu.SemaphoreType.DMA
    scratch = dict(
        tokens_v=V((T, D), BF16), og_v=V((T, D), BF16), wq_v=V((L, D), BF16), wk_v=V((L, D), BF16),
        wv_v=V((L, D), BF16), wo_v=V((L, D), BF16), wu_v=V((D, F), BF16), wd_v=V((F, D), BF16), vecs=V((9, D), F32),
        q=V((T, L), BF16), k=V((T, L), BF16), v=V((T, L), BF16), ctx=V((T, L), BF16),
        dq=V((T, L), BF16), dk=V((T, L), BF16), dv=V((T, L), BF16), dk_acc=V((S, L), F32), dv_acc=V((S, L), F32),
        probs=V((NC * heads, QB, KW), BF16),
        xhat1=V((NC, half, D), F32), xhat2=V((NC, half, D), F32), hid=V((NC, half, D), F32), d2=V((NC, half, D), F32),
        d1=V((NC, half, D), F32), rstd1=V((NC, half, 1), F32), rstd2=V((NC, half, 1), F32),
        rest=V((half, D), BF16), dtok=V((half, D), F32),
        hl=V((T, D), BF16), act=V((T, F), BF16), gp=V((T, F), BF16), d2l=V((T, D), BF16), dup=V((T, F), BF16),
        d1l=V((T, D), BF16),
        part=V((2, NC, QB, D), BF16), arecv=V((2, NC, half, D), BF16),
        ysend=V((2, NC, half, D), BF16), yrecv=V((2, NC, half, D), BF16),
        pool=V((16, D), F32), pool_r=V((16, D), F32), dpool=V((16, D), F32), acc=V((9, 8, D), F32),
        outg=V((n_dp * 16, 128), BF16), inc=V((n_dp * 16, 128), BF16), outg2=V((n_dp * 16, 128), BF16),
        inc2=V((n_dp * 16, 128), BF16),
        vmine=V((8, D), F32), vsib=V((8, D), F32), vg=V((16, D // 2), BF16), vr=V((3, 16, D // 2), BF16),
        grad=V((3, D, D), BF16), rx=V((rx_rows, D), BF16),
        in_sem=dma((8,)), a_s=dma((2,)), a_r=dma((2, NC)), y_s=dma((2, NC)), y_r=dma((2, NC)),
        g_s=dma((5,)), g_r=dma((3, NC)), pool_sem=dma((4,)), p_s=dma((n_dp,)), p_r=dma((2, n_dp)),
        v_s=dma((2,)), v_r=dma((3,)), d_s=dma((n_slots, 2)), d_r=dma((n_jobs, 4)),
    )
    names = tuple(ins) + tuple(outs) + tuple(scratch)
    res, tg, grads, vec, loss = pl.pallas_call(
        functools.partial(layer_kernel, z, names),
        out_shape=[V(*s) for s in outs.values()],
        in_specs=in_specs,
        out_specs=[vmem] * 5,
        scratch_shapes=list(scratch.values()),
        compiler_params=pltpu.CompilerParams(
            collective_id=0, has_side_effects=True, vmem_limit_bytes=VMEM1
        ),
    )(*ins.values())
    if not z.in_kernel:
        grads, vec = lax.psum((grads, vec), "dp")
    un_outs = [((F, D), F32), ((D, F), F32), ((T, D), BF16), ((T, D), F32)] + [((L, D), F32)] * 4
    n_big = len(un_outs)
    un_outs += [((D,), F32)] * 7 + [((L,), F32)] * 2 + [((R * 3,), F32)]
    o = pl.pallas_call(
        functools.partial(unpack_kernel, z),
        out_shape=[jax.ShapeDtypeStruct(*s) for s in un_outs],
        in_specs=[vmem] * 5,
        out_specs=[any_] * n_big + [vmem] * (len(un_outs) - n_big),
        scratch_shapes=[V((3, D, D), F32), dma((6 + 3 * (D // L),))],
        compiler_params=pltpu.CompilerParams(vmem_limit_bytes=24 * 2**20),
    )(grads, res, tg, vec, loss)
    gd, gu, res, tg, gq, gk, gv, go, v0, v1, v2, v3, v4, v5, v6, bq, bv, loss = o
    return res, loss, tg, gq.T, bq, gk.T, gv.T, bv, go, v0, v1, v2, gu, v6, gd, v3, v4, v5


def solution(mesh):
    rows, flat, cut = P("dp", None), P("dp"), P("mp")
    across, down = P(None, "mp"), P("mp", None)
    return jax.shard_map(
        functools.partial(on_device, mesh.shape["dp"]),
        mesh=mesh,
        in_specs=(rows, rows, flat, flat, across, cut, across, across, cut, down, P(), P(), P(), across, cut, down,
                  P(), P(), P(), rows),
        out_specs=(rows, flat, rows, across, cut, across, across, cut, down, P(), P(), P(), across, cut, down, P(),
                   P(), P()),
        check_vma=False,
    )
```

```python
import functools
import types

import jax
import jax.numpy as jnp
from jax import lax
from jax.experimental import pallas as pl
from jax.experimental.pallas import tpu as pltpu
from jax.sharding import PartitionSpec as P

HEAD_DIM = 64
MAX_PIECE = 128
NEG_FILL = -1e30
NORM_EPS = 1e-12
UNIT_EPS = 1e-06
SIM_SCALE = 50.0
MESH = pl.DeviceIdType.MESH
F32, BF16, I32 = jnp.float32, jnp.bfloat16, jnp.int32
HIGHEST = lax.Precision.HIGHEST


def nn(a, b):
    return lax.dot_general(a, b, (((1,), (0,)), ((), ())), preferred_element_type=F32)


def nt(a, b):
    return lax.dot_general(a, b, (((1,), (1,)), ((), ())), preferred_element_type=F32)


def tn(a, b):
    return lax.dot_general(a, b, (((0,), (0,)), ((), ())), preferred_element_type=F32)


def iota(shape, axis):
    return lax.broadcasted_iota(I32, shape, axis)


def hi_lo(x):
    hi = x.astype(BF16).astype(F32)
    return hi, x - hi


def layer_kernel(z, names, *refs):
    ns = types.SimpleNamespace(**dict(zip(names, refs)))
    n_dp, R, S, D, L, F, heads = z.n_dp, z.R, z.S, z.D, z.L, z.F, z.heads
    QB, KW = z.QB, z.KW
    n_qb, half = S // QB, QB // 2
    NC = R * n_qb
    CH = D // 128
    dp, mp = lax.axis_index("dp"), lax.axis_index("mp")
    core = mp % 2
    other = 1 - core
    sib = (dp, mp + 1 - 2 * core)
    across = (dp, (mp + 2) % 4)
    diagonal = (dp, (mp + 3 - 2 * core) % 4)

    bar = pltpu.get_barrier_semaphore()
    for t in (sib, across, diagonal):
        pl.semaphore_signal(bar, inc=1, device_id=t, device_id_type=MESH)
    for d in range(1, n_dp):
        pl.semaphore_signal(bar, inc=1, device_id=((dp + d) % n_dp, mp), device_id_type=MESH)

    loads = []
    for i, (src, dst) in enumerate((
        (ns.wo, ns.wo_all.at[mp]), (ns.tokens, ns.tokens_v), (ns.wq, ns.wq_v), (ns.wk, ns.wk_v), (ns.wv, ns.wv_v),
        (ns.wu, ns.wu_v), (ns.wd, ns.wd_v), (ns.og, ns.og_v),
    )):
        loads.append(pltpu.make_async_copy(src, dst, ns.in_sem.at[i]))
        loads[-1].start()
    vecs = ns.vecs
    for i, x in enumerate((
        ns.b_query, ns.b_value, ns.output_bias, ns.first_norm_gain, ns.first_norm_bias, ns.b_up, ns.down_bias,
        ns.second_norm_gain, ns.second_norm_bias,
    )):
        n = x.shape[0]
        vecs[i : i + 1, 0:n] = x[...].reshape(1, n)
    pl.semaphore_wait(bar, 2 + n_dp)

    sends = []

    def remote(src, dst, ss, rs, to):
        return pltpu.make_async_remote_copy(
            src_ref=src, dst_ref=dst, send_sem=ss, recv_sem=rs, device_id=to, device_id_type=MESH
        )

    def vec(i, n=None):
        return vecs[i : i + 1, : (n or D)]

    ends = []
    for r in range(R):
        total, row = 0, []
        for p in range(7):
            total = total + ns.lengths[r, p]
            row.append(total)
        ends.append(row)

    def seg_of(position, r):
        seg = jnp.zeros(position.shape, I32)
        for p in range(6):
            seg = seg + jnp.where(position >= ends[r][p], 1, 0)
        return seg

    lane_head = iota((1, L), 1) // HEAD_DIM

    def only_head(x, h):
        return jnp.where(lane_head == h, x, jnp.zeros_like(x))

    in_flight = {}
    unsent = {}

    def finish_send(key):
        if key in unsent:
            sem, copy = unsent.pop(key)
            copy.wait_send()
            del in_flight[sem]

    def begin_send(key, sem, copy):
        if sem in in_flight:
            finish_send(in_flight[sem])
        in_flight[sem] = key
        unsent[key] = (sem, copy)
        copy.start()

    def pair_copy(which, c):
        par = which % 2
        return remote(ns.part.at[par, c, pl.ds(pl.multiple_of(other * half, half), half)], ns.arecv.at[par, c],
                      ns.a_s.at[par, c], ns.a_r.at[par, c], sib)

    def cross_copy(which, c):
        par = which % 2
        return remote(ns.ysend.at[par, c], ns.yrecv.at[par, c], ns.y_s.at[par, c], ns.y_r.at[par, c], across)

    def send_part(which, c, compute):
        part = ns.part.at[which % 2, c]

        def put(cols, val):
            part[:, cols] = val.astype(BF16)

        if which >= 2:
            finish_send((0, which - 2, c))
        compute(c, put)
        begin_send((0, which, c), (0, which % 2, c), pair_copy(which, c))

    def send_across(which, c):
        par = which % 2
        pair_copy(which, c).wait_recv()
        if which >= 2:
            finish_send((1, which - 2, c))
        own = pl.ds(pl.multiple_of(core * half, half), half)
        ns.ysend[par, c] = ns.part[par, c, own] + ns.arecv[par, c]
        begin_send((1, which, c), (1, which % 2, c), cross_copy(which, c))

    def y_total(which, c, rows):
        par = which % 2
        return ns.ysend[par, c, rows].astype(F32) + ns.yrecv[par, c, rows].astype(F32)

    def at_chunk(c):
        return slice(c * QB, c * QB + QB)

    def halves(i, c):
        rows = pl.ds(pl.multiple_of(c * QB + core * half, half), half)
        x = (ns.hl, ns.res, ns.d2l, ns.d1l, ns.tg)[i]
        return remote(x.at[rows], x.at[rows], ns.g_s.at[i, c], ns.g_r.at[G_SLOT[i], c], sib)

    def to_sibling(i, c):
        begin_send((2, i, c), (2, i, c), halves(i, c))

    TR = z.TR

    def by_rows(fn):
        def body(i, _):
            fn(pl.ds(pl.multiple_of(i * TR, TR), TR), i * TR)
            return 0

        lax.fori_loop(0, half // TR, body, 0, unroll=z.unroll)

    def fold(x):
        return jnp.sum(x.reshape(x.shape[0] // 8, 8, x.shape[1]), axis=0)

    def row_ds(c, start, n):
        return pl.ds(pl.multiple_of(c * QB + core * half + start, n), n)

    def columns(width, step=256):
        return [slice(n, n + step) for n in range(0, width, step)]

    def project(r):
        rows = pl.ds(r * S, S)
        x = ns.tokens_v[rows, :]
        ns.q[rows, :] = ((nt(x, ns.wq_v[...]) + vec(0, L)).astype(BF16) * (HEAD_DIM**-0.5)).astype(BF16)
        ns.k[rows, :] = nt(x, ns.wk_v[...]).astype(BF16)
        ns.v[rows, :] = (nt(x, ns.wv_v[...]) + vec(1, L)).astype(BF16)

    def win(b):
        return min(max(b * QB - MAX_PIECE, 0), S - KW)

    def attend(c):
        r, b = c // n_qb, c % n_qb
        q0, k0 = c * QB, r * S + win(b)
        same = seg_of(iota((QB, 1), 0) + b * QB, r) == seg_of(iota((1, KW), 1) + win(b), r)
        qb = ns.q[q0 : q0 + QB, :]
        kb = ns.k[k0 : k0 + KW, :]
        vb = ns.v[k0 : k0 + KW, :]
        ctx = None
        for h in range(heads):
            s = jnp.where(same, nt(only_head(qb, h), kb), NEG_FILL)
            e = jnp.exp(s - jnp.max(s, axis=-1, keepdims=True))
            p = (e * (1.0 / jnp.sum(e, axis=-1, keepdims=True))).astype(BF16)
            ns.probs[c * heads + h] = p
            o = nn(p, only_head(vb, h))
            ctx = o if ctx is None else ctx + o
        ns.ctx[q0 : q0 + QB, :] = ctx.astype(BF16)

    def weight_copy(k):
        if k == 2:
            x = ns.wo_all.at[(mp + 2) % 4]
        else:
            x = ns.wo_all.at[mp]
        return remote(x, x, ns.w_s.at[k], ns.w_r.at[k], (sib, across, sib)[k])

    def context_copy(c, k):
        mine = k == 1
        rows = pl.ds(pl.multiple_of(c * QB + (core if mine else other) * half, half), half)
        return remote(ns.ctx.at[rows], ns.ctx_all.at[c, mp], ns.cx_s.at[c, k], ns.cx_r.at[c, k], (sib, across, diagonal)[k])

    def send_context(c):
        for k in (1, 2, 0):
            context_copy(c, k).start()
            sends.append(context_copy(c, k))
        ns.ctx_all[c, mp] = ns.ctx[row_ds(c, 0, half), :]

    def attn_out(c):
        for w in columns(D):
            total = nn(ns.ctx_all[c, 0], ns.wo_all[0, :, w])
            for k in range(1, 4):
                total = total + nn(ns.ctx_all[c, k], ns.wo_all[k, :, w])
            ns.dtok[:, w] = total

    def norm(v):
        mean = jnp.mean(v, axis=-1, keepdims=True)
        d = v - mean
        rstd = lax.rsqrt(jnp.mean(d * d, axis=-1, keepdims=True) + NORM_EPS)
        return d * rstd, rstd

    def first_norm(c):
        def body(rows, start):
            mine = row_ds(c, start, TR)
            xh, rstd = norm(ns.tokens_v[mine].astype(F32) + ns.dtok[rows] + vec(2))
            ns.xhat1[c, rows] = xh
            ns.rstd1[c, rows] = rstd
            h = xh * vec(3) + vec(4)
            ns.hid[c, rows] = h
            ns.hl[mine] = h.astype(BF16)

        by_rows(body)

    def ffn_up(c):
        x = ns.hl[at_chunk(c), :]
        for w in columns(F):
            u = nn(x, ns.wu_v[:, w]) + vecs[5:6, w]
            phi = 0.5 + 0.5 * lax.erf(u * 0.7071067811865476)
            ns.act[at_chunk(c), w] = (u * phi).astype(BF16)
            ns.gp[at_chunk(c), w] = (phi + u * (jnp.exp(-0.5 * (u * u)) * 0.3989422804014327)).astype(BF16)

    def ffn_down(c, put):
        x = ns.act[at_chunk(c), :]
        for w in columns(D):
            put(w, nn(x, ns.wd_v[:, w]))

    def second_norm(c):
        r, b = c // n_qb, c % n_qb

        def body(rows, start):
            xh, rstd = norm(ns.hid[c, rows] + y_total(1, c, rows) + vec(6))
            ns.xhat2[c, rows] = xh
            ns.rstd2[c, rows] = rstd
            res = xh * vec(7) + vec(8)
            low = res.astype(BF16)
            ns.res[row_ds(c, start, TR)] = low
            ns.rest[rows] = (res - low.astype(F32)).astype(BF16)

        by_rows(body)
        piece = iota((8, half), 0)
        seg = seg_of(iota((8, half), 1) + (core * half + b * QB), r)
        member = jnp.where((seg == piece) & (piece < 6), 1.0, 0.0).astype(BF16)
        at = slice(r * 8, r * 8 + 8)
        ns.pool[at, :] += nn(member, ns.res[row_ds(c, 0, half)]) + nn(member, ns.rest[...])

    PR = 16
    n_sent = R * 6

    def per_row(values, axis, shape, fill):
        pos = iota(shape, axis) % PR
        out = jnp.full(shape, fill, I32)
        for s in range(n_sent):
            out = jnp.where(pos == (s // 6) * 8 + s % 6, values[s], out)
        return out

    def slot_onehot(axis):
        shape = (n_dp * 16, CH * PR) if axis == 1 else (CH * PR, n_dp * 16)
        line = (1, CH * PR) if axis == 1 else (CH * PR, 1)
        vals = [ns.send_slot[s] // 2 * 16 + ns.send_slot[s] % 2 for s in range(n_sent)]
        target = per_row(vals, axis if axis == 1 else 0, line, -65536) + iota(line, 1 if axis == 1 else 0) // PR * 2
        return jnp.where(iota(shape, 0 if axis == 1 else 1) == target, 1.0, 0.0).astype(BF16)

    def place_onehot(axis):
        line = (1, n_dp * 16) if axis == 1 else (n_dp * 16, 1)
        shape = (CH * PR, n_dp * 16) if axis == 1 else (n_dp * 16, CH * PR)
        pos = iota(line, axis)
        slot = pos // 16 * 2 + pos % 2
        target = jnp.zeros(line, I32)
        for s in range(2 * n_dp):
            target = jnp.where(slot == s, ns.recv_place[s], target)
        target = target + pos % 16 // 2 * PR
        return jnp.where(iota(shape, 0 if axis == 1 else 1) == target, 1.0, 0.0).astype(BF16)

    def stack(x):
        return jnp.concatenate([x[:, c * 128 : c * 128 + 128] for c in range(CH)], axis=0)

    def unstack(x):
        return jnp.concatenate([x[c * PR : c * PR + PR] for c in range(CH)], axis=1)

    def peers(src, dst, ssem, rsem):
        cs = []
        mine = pl.ds(pl.multiple_of(dp * 16, 16), 16)
        for d in range(1, n_dp):
            t = (dp + d) % n_dp
            c = remote(src.at[pl.ds(pl.multiple_of(t * 16, 16), 16)], dst.at[mine], ssem.at[d], rsem.at[d], (t, mp))
            c.start()
            cs.append(c)
        dst[mine] = src[mine]
        for c in cs:
            c.wait()

    def pairs():
        c = remote(ns.pool, ns.pool_r, ns.pool_sem.at[0], ns.pool_sem.at[1], sib)
        c.start()
        lens = [ns.lengths[s // 6, s % 6] for s in range(n_sent)]
        size = per_row(lens, 0, (PR, 1), 1).astype(F32)
        inv = 1.0 / size
        hot = slot_onehot(1)
        c.wait()
        pooled = (ns.pool[...] + ns.pool_r[...]) * inv
        ns.outg[...] = nn(hot, stack(pooled).astype(BF16)).astype(BF16)
        peers(ns.outg, ns.inc, ns.p_s, ns.p_r.at[0])
        o = unstack(nn(place_onehot(1), ns.inc[...]))
        s = lax.rsqrt(jnp.sum(o * o, axis=-1, keepdims=True) + UNIT_EPS)
        u = o * s
        logits = SIM_SCALE * lax.dot_general(
            u, u, (((1,), (1,)), ((), ())), precision=HIGHEST, preferred_element_type=F32
        )
        i, j = iota((PR, PR), 0), iota((PR, PR), 1)
        live = (i % 2 == 0) & (i < n_sent) & (j % 2 == 1) & (j < n_sent)
        lm = jnp.where(live, logits, NEG_FILL)
        peak = jnp.max(lm, axis=-1, keepdims=True)
        e = jnp.where(live, jnp.exp(lm - peak), 0.0)
        tot = jnp.maximum(jnp.sum(e, axis=-1, keepdims=True), 1e-30)
        partner = live & (j == i + 1)
        loss = peak + jnp.log(tot) - jnp.sum(jnp.where(partner, logits, 0.0), axis=-1, keepdims=True)
        i2, j2 = iota((PR, 128), 0), iota((PR, 128), 1)
        ns.loss_v[...] = jnp.broadcast_to(
            jnp.sum(jnp.where((i2 == 2 * j2) & (i2 < n_sent), loss, 0.0), axis=0, keepdims=True), (8, 128)
        )
        dl = e / tot - jnp.where(partner, 1.0, 0.0)
        du = SIM_SCALE * (
            lax.dot_general(dl, u, (((1,), (0,)), ((), ())), precision=HIGHEST, preferred_element_type=F32)
            + lax.dot_general(dl, u, (((0,), (0,)), ((), ())), precision=HIGHEST, preferred_element_type=F32)
        )
        do = s * (du - u * jnp.sum(u * du, axis=-1, keepdims=True))
        ns.outg2[...] = nn(place_onehot(0), stack(do).astype(BF16)).astype(BF16)
        peers(ns.outg2, ns.inc2, ns.p_s, ns.p_r.at[1])
        ns.dpool[...] = unstack(nn(slot_onehot(0), ns.inc2[...])) * inv

    def norm_back(dx, xh, rstd):
        return rstd * (
            dx - jnp.mean(dx, axis=-1, keepdims=True) - xh * jnp.mean(dx * xh, axis=-1, keepdims=True)
        )

    def second_norm_back(c):
        r, b = c // n_qb, c % n_qb
        hi, lo = hi_lo(ns.dpool[r * 8 : r * 8 + 8, :])
        lane = iota((half, 16), 1) % 8
        seg = seg_of(iota((half, 1), 0) + (core * half + b * QB), r)
        member = jnp.where((seg == lane) & (lane < 6), 1.0, 0.0).astype(BF16)
        ns.dtok[...] = nn(member, jnp.concatenate([hi, lo], axis=0).astype(BF16))

        def body(rows, start):
            mine = row_ds(c, start, TR)
            d = ns.og_v[mine].astype(F32) + ns.dtok[rows]
            xh = ns.xhat2[c, rows]
            ns.acc[4] += fold(d * xh)
            ns.acc[5] += fold(d)
            d2 = norm_back(d * vec(7), xh, ns.rstd2[c, rows])
            ns.acc[3] += fold(d2)
            ns.d2[c, rows] = d2
            ns.d2l[mine] = d2.astype(BF16)

        by_rows(body)

    def ffn_back(c):
        rows = at_chunk(c)
        x = ns.d2l[rows, :]
        for w in columns(F):
            da = nt(x, ns.wd_v[w, :]).astype(BF16)
            du = (da.astype(F32) * ns.gp[rows, w].astype(F32)).astype(BF16)
            ns.dup[rows, w] = du
            ns.acc[6, :, w] += fold(du.astype(F32))

    def ffn_back_out(c, put):
        x = ns.dup[at_chunk(c), :]
        for w in columns(D):
            put(w, nt(x, ns.wu_v[w, :]))

    def down_weights(n):
        for w in columns(F)[n : n + 1]:
            grad[0, w, :] = tn(ns.act[:, w], ns.d2l[...]).astype(BF16)

    def up_weights(n):
        for w in columns(D)[n : n + 1]:
            grad[1, w, :] = tn(ns.hl[:, w], ns.dup[...]).astype(BF16)

    def first_norm_back(c):
        def body(rows, start):
            mine = row_ds(c, start, TR)
            d = ns.d2[c, rows] + y_total(2, c, rows)
            xh = ns.xhat1[c, rows]
            ns.acc[1] += fold(d * xh)
            ns.acc[2] += fold(d)
            d1 = norm_back(d * vec(3), xh, ns.rstd1[c, rows])
            ns.acc[0] += fold(d1)
            ns.d1[c, rows] = d1
            ns.d1l[mine] = d1.astype(BF16)

        by_rows(body)

    def attend_back(c):
        r, b = c // n_qb, c % n_qb
        q0, k0 = c * QB, r * S + win(b)
        cb = nt(ns.d1l[at_chunk(c), :], ns.wo_all[mp]).astype(BF16)
        qb = ns.q[q0 : q0 + QB, :]
        kb = ns.k[k0 : k0 + KW, :]
        vb = ns.v[k0 : k0 + KW, :]
        dq = dk = dv = None
        for h in range(heads):
            p = ns.probs[c * heads + h]
            dp_ = nt(cb, only_head(vb, h))
            pf = p.astype(F32)
            delta = jnp.sum(pf * dp_, axis=-1, keepdims=True)
            ds = (pf * (dp_ - delta)).astype(BF16)
            t, u, w = nn(ds, only_head(kb, h)), tn(ds, only_head(qb, h)), tn(p, only_head(cb, h))
            dq, dk, dv = (t, u, w) if dq is None else (dq + t, dk + u, dv + w)
        dq = (dq * (HEAD_DIM**-0.5)).astype(BF16)
        ns.dq[q0 : q0 + QB, :] = dq
        ns.acc[7, :, :L] += fold(dq.astype(F32))
        at = slice(win(b), win(b) + KW)
        if b == 0:
            ns.dk_acc[...] = jnp.zeros((S, L), F32)
            ns.dv_acc[...] = jnp.zeros((S, L), F32)
        ns.dk_acc[at, :] += dk
        ns.dv_acc[at, :] += dv
        if b == n_qb - 1:
            rows = slice(r * S, r * S + S)
            ns.dk[rows, :] = ns.dk_acc[...].astype(BF16)
            dvr = ns.dv_acc[...].astype(BF16)
            ns.dv[rows, :] = dvr
            ns.acc[8, :, :L] += fold(dvr.astype(F32))

    def attend_back_out(c, put):
        at = at_chunk(c)
        for w in columns(D):
            put(
                w,
                nn(ns.dq[at, :], ns.wq_v[:, w])
                + nn(ns.dk[at, :], ns.wk_v[:, w])
                + nn(ns.dv[at, :], ns.wv_v[:, w]),
            )

    def attend_weights():
        for i, x in enumerate((ns.dq, ns.dk, ns.dv)):
            grad[2, i * L : i * L + L, :] = tn(x[...], ns.tokens_v[...]).astype(BF16)
        grad[2, 3 * L : 4 * L, :] = tn(ns.ctx[...], ns.d1l[...]).astype(BF16)

    def finish(c):
        def body(rows, start):
            ns.tg[row_ds(c, start, TR)] = ns.d1[c, rows] + y_total(3, c, rows)

        by_rows(body)

    xi, zi = dp % 2, dp // 2
    nz = n_dp // 2
    in_kernel = z.in_kernel
    outer = (zi == 0) | (zi == nz - 1)
    inner = (zi != 0) & (zi != nz - 1)
    xp = (dp + 1 - 2 * xi, mp)
    zp = (dp + 2 - 4 * (zi % 2), mp)
    zq = ((dp + 2 * (3 - 2 * zi)) % n_dp if in_kernel else dp, mp)
    ii = zi // 2
    grad, gsum = ns.grad, ns.gsum

    def when(condition, fn):
        return lambda: pl.when(condition)(fn)

    def add_into(dst, dst_at, a_at, b_at, n):
        step = 48 if n % 48 == 0 else 32 if n % 32 == 0 else 16

        def body(i, _):
            o = i * step
            x = grad[a_at[0], pl.ds(pl.multiple_of(a_at[1] + o, 16), step), :]
            y = ns.rx[pl.ds(pl.multiple_of(b_at + o, 16), step), :]
            dst[dst_at[0], pl.ds(pl.multiple_of(dst_at[1] + o, 16), step), :] = x + y
            return 0

        lax.fori_loop(0, n // step, body, 0)

    def x_job(slot, j, r0, n):
        h = n // 2
        mine = pl.multiple_of(r0 + xi * h, 16)
        yours = pl.multiple_of(r0 + (1 - xi) * h, 16)
        own, theirs = pl.ds(mine, h), pl.ds(yours, h)
        s = lambda k: ns.d_s.at[z.slots[slot], k]
        q = lambda k: ns.d_r.at[slot, k]
        b0 = z.rx_at[slot]
        buf = lambda k: ns.rx.at[pl.ds(b0 + k * h, h)]
        x1 = remote(grad.at[j, theirs], buf(0), s(0), q(0), xp)
        z1 = remote(grad.at[j, own], buf(1), s(0), q(1), zp)
        z2 = remote(grad.at[j, own], buf(2), s(0), q(2), zq)
        z3 = remote(gsum.at[j, own], gsum.at[j, own], s(1), q(1), zp)
        x2 = remote(gsum.at[j, own], gsum.at[j, own], s(0), q(3), xp)

        def s1o():
            x1.wait()
            add_into(grad, (j, mine), (j, mine), b0, h)
            z1.start()

        def s1i():
            x1.wait()
            add_into(grad, (j, mine), (j, mine), b0, h)

        def s2():
            z1.wait_recv()
            add_into(grad, (j, mine), (j, mine), b0 + h, h)
            z2.start()

        def s3():
            z2.wait()
            add_into(gsum, (j, mine), (j, mine), b0 + 2 * h, h)
            z3.start()
            x2.start()

        def s4():
            z3.wait_recv()
            z1.wait_send()
            x2.start()

        def end():
            x2.wait_send()
            pl.when(inner)(z3.wait_send)

        steps = {0: x1.start, 1: when(outer, s1o), 8: when(inner, s1i), 2: when(inner, s2), 3: when(inner, s3),
                 4: when(outer, s4), 5: x2.wait_recv}
        return steps, end

    def z_job(slot, j, r0, n):
        h = n // 2
        mine = pl.multiple_of(r0 + ii * h, 16)
        yours = pl.multiple_of(r0 + (1 - ii) * h, 16)
        own, theirs, whole = pl.ds(mine, h), pl.ds(yours, h), pl.ds(r0, n)
        s = lambda k: ns.d_s.at[z.slots[slot], k]
        q = lambda k: ns.d_r.at[slot, k]
        b0 = z.rx_at[slot]
        buf = lambda k: ns.rx.at[pl.ds(b0 + k * h, h)]
        z1 = remote(grad.at[j, whole], ns.rx.at[pl.ds(b0 + n, n)], s(0), q(0), zp)
        z2 = remote(grad.at[j, theirs], buf(0), s(0), q(1), zq)
        x = remote(grad.at[j, own], buf(1), s(1), q(2), xp)
        z2b = remote(gsum.at[j, own], gsum.at[j, own], s(0), q(3), zq)
        z3a = remote(gsum.at[j, own], gsum.at[j, own], s(1), q(1), zp)
        z3b = remote(gsum.at[j, theirs], gsum.at[j, theirs], s(0), q(2), zp)

        def s1():
            z1.wait_recv()
            add_into(grad, (j, r0), (j, r0), b0 + n, n)
            z2.start()

        def s2():
            z2.wait_recv()
            add_into(grad, (j, mine), (j, mine), b0, h)
            x.start()

        def s3():
            x.wait()
            z2.wait_send()
            add_into(gsum, (j, mine), (j, mine), b0 + h, h)
            z2b.start()
            z3a.start()

        def s4():
            z2b.wait()
            z3b.start()

        def s5():
            z3a.wait_recv()
            z3b.wait_recv()

        def end():
            pl.when(outer)(z1.wait_send)

            @pl.when(inner)
            def _():
                z3a.wait_send()
                z3b.wait_send()

        steps = {0: when(outer, z1.start), 1: when(inner, s1), 2: when(inner, s2), 3: when(inner, s3),
                 4: when(inner, s4), 5: when(outer, s5)}
        return steps, end

    def q_job(slot, j, r0, n):
        h, f = n // 2, n // 4
        mine = pl.multiple_of(r0 + ii * h, 16)
        yours = pl.multiple_of(r0 + (1 - ii) * h, 16)
        own, theirs, whole = pl.ds(mine, h), pl.ds(yours, h), pl.ds(r0, n)
        back_a = pl.ds(pl.multiple_of(mine + xi * f, 16), f)
        back_b = pl.ds(pl.multiple_of(yours + xi * f, 16), f)
        s = lambda k: ns.d_s.at[z.slots[slot], k]
        q = lambda k: ns.d_r.at[slot, k]
        b0 = z.rx_at[slot]
        buf = lambda k: ns.rx.at[pl.ds(b0 + k * h, h)]
        z1 = remote(grad.at[j, whole], ns.rx.at[pl.ds(b0 + n, n)], s(0), q(0), zp)
        z2 = remote(grad.at[j, theirs], buf(0), s(0), q(1), zq)
        x = remote(grad.at[j, own], buf(1), s(1), q(2), xp)
        z2b = remote(gsum.at[j, own], gsum.at[j, own], s(0), q(3), zq)
        z3a = remote(gsum.at[j, back_a], gsum.at[j, back_a], s(1), q(0), zp)
        z3b = remote(gsum.at[j, back_b], gsum.at[j, back_b], s(0), q(1), zp)
        xa = remote(gsum.at[j, back_a], gsum.at[j, back_a], s(0), q(2), xp)
        xb = remote(gsum.at[j, back_b], gsum.at[j, back_b], s(1), q(3), xp)

        def s1():
            z1.wait_recv()
            add_into(grad, (j, r0), (j, r0), b0 + n, n)
            z2.start()

        def s2():
            z2.wait_recv()
            add_into(grad, (j, mine), (j, mine), b0, h)
            x.start()

        def s3():
            x.wait()
            z2.wait_send()
            add_into(gsum, (j, mine), (j, mine), b0 + h, h)
            z2b.start()
            z3a.start()

        def s4():
            z2b.wait()
            z3b.start()

        def s5():
            z3a.wait_recv()
            z1.wait_send()
            xa.start()
            z3b.wait_recv()
            xb.start()

        def s6():
            xa.wait_recv()
            xb.wait_recv()

        def end():
            @pl.when(outer)
            def _():
                xa.wait_send()
                xb.wait_send()

            @pl.when(inner)
            def _():
                z3a.wait_send()
                z3b.wait_send()

        steps = {0: when(outer, z1.start), 1: when(inner, s1), 2: when(inner, s2), 3: when(inner, s3),
                 4: when(inner, s4), 5: when(outer, s5), 6: when(outer, s6)}
        return steps, end

    def u_job(slot, j, r0, n):
        near = pl.multiple_of(r0 + ii * n, 16)
        far = pl.multiple_of(r0 + (1 - ii) * n, 16)
        near_d, far_d = pl.ds(near, n), pl.ds(far, n)
        s = lambda k: ns.d_s.at[z.slots[slot], k]
        q = lambda k: ns.d_r.at[slot, k]
        b0 = z.rx_at[slot]
        buf = lambda k: ns.rx.at[pl.ds(b0 + k * n, n)]
        za = remote(grad.at[j, far_d], buf(0), s(0), q(0), zp)
        ma = remote(grad.at[j, far_d], buf(1), s(0), q(1), zq)
        zb = remote(grad.at[j, near_d], buf(0), s(1), q(0), zp)
        xa = remote(grad.at[j, near_d], buf(1), s(1), q(1), xp)
        zc = remote(gsum.at[j, near_d], gsum.at[j, near_d], s(0), q(2), zp)
        mb = remote(gsum.at[j, near_d], gsum.at[j, near_d], s(0), q(3), zq)
        zd = remote(gsum.at[j, far_d], gsum.at[j, far_d], s(1), q(2), zp)

        def s1():
            za.wait_recv()
            add_into(grad, (j, far), (j, far), b0, n)
            ma.start()

        def s2():
            ma.wait_recv()
            add_into(grad, (j, near), (j, near), b0 + n, n)
            zb.start()

        def s3():
            zb.wait_recv()
            add_into(grad, (j, near), (j, near), b0, n)
            xa.start()

        def s4():
            xa.wait_recv()
            za.wait_send()
            add_into(gsum, (j, near), (j, near), b0 + n, n)
            zc.start()

        def s5():
            zc.wait_recv()
            ma.wait_send()
            mb.start()

        def s6():
            mb.wait_recv()
            zb.wait_send()
            zd.start()

        def end():
            @pl.when(outer)
            def _():
                xa.wait_send()
                zc.wait_send()

            @pl.when(inner)
            def _():
                mb.wait_send()
                zd.wait_send()

        steps = {0: when(outer, za.start), 1: when(inner, s1), 2: when(inner, s2), 3: when(outer, s3),
                 4: when(outer, s4), 5: when(inner, s5), 6: when(inner, s6), 7: when(outer, zd.wait_recv)}
        return steps, end

    def vector_job():
        vg, vr = ns.vg, ns.vr
        s = lambda k: ns.v_s.at[k]
        q = lambda k: ns.v_r.at[k]
        z1 = remote(vg, vr.at[0], s(0), q(0), zp)
        z2 = remote(vg, vr.at[1], s(0), q(1), zq)
        x = remote(vg, vr.at[2], s(1), q(2), xp)
        z3 = remote(ns.vt, ns.vt, s(0), q(0), zp)

        def c1():
            z1.wait_recv()
            vg[...] = vg[...] + vr[0]
            z2.start()

        def c2():
            z2.wait_recv()
            z2.wait_send()
            vg[...] = vg[...] + vr[1]
            x.start()

        def c3():
            x.wait_recv()
            ns.vt[...] = vg[...] + vr[2]
            z3.start()

        def end():
            pl.when(outer)(z1.wait_send)

            @pl.when(inner)
            def _():
                x.wait_send()
                z3.wait_send()

        steps = {0: when(outer, z1.start), 1: when(inner, c1), 2: when(inner, c2), 3: when(inner, c3),
                 4: when(outer, z3.wait_recv)}
        return steps, end

    tasks, ends_of = {}, {}
    if in_kernel:
        for i, (kind, j, r0, n) in enumerate(z.jobs):
            steps, end = (x_job, z_job, q_job, u_job)[kind](i, j, r0, n)
            tasks.update({JOB + i * 10 + k: f for k, f in steps.items()})
            ends_of[i] = end
        steps, end = vector_job()
        tasks.update({VECTOR + k: f for k, f in steps.items()})
        ends_of[-1] = end

    waited = set()

    def once(key, fn):
        if key not in waited:
            waited.add(key)
            fn()

    def load(*keys):
        for k in keys:
            once((9, k), loads[k].wait)

    def come(i, c):
        once((i, c), halves(i, c).wait_recv)

    load(0)
    for k in (1, 0):
        weight_copy(k).start()
        sends.append(weight_copy(k))
    ns.pool[...] = jnp.zeros((PR, D), F32)
    ns.acc[...] = jnp.zeros(ns.acc.shape, F32)

    def run_project(r):
        load(1, 2, 3, 4)
        project(r)

    def run_relay(_):
        weight_copy(1).wait_recv()
        weight_copy(2).start()
        sends.append(weight_copy(2))

    def run_norm(c):
        for k in range(3):
            context_copy(c, k).wait_recv()
        for k in (0, 2):
            once((8, k), weight_copy(k).wait_recv)
        attn_out(c)
        first_norm(c)
        to_sibling(0, c)

    def run_up(c):
        load(5)
        come(0, c)
        ffn_up(c)

    def run_down(c):
        load(6)
        send_part(1, c, ffn_down)

    def run_second(c):
        cross_copy(1, c).wait_recv()
        second_norm(c)
        to_sibling(1, c)

    forward = (run_project, attend, send_context, run_relay, run_norm, run_up, run_down,
               functools.partial(send_across, 1), run_second)
    if NC == 4:
        plan = FORWARD
    else:
        plan = [r for r in range(R)]
        plan += [10 * k + c for c in range(NC) for k in (1, 2)] + [30]
        for group in ((4, 5, 6, 7), (8,)):
            plan += [10 * k + c for c in range(NC) for k in group]
    for k in plan:
        forward[k // 10](k % 10)
    load(7)
    pairs()

    def run_second_back(c):
        second_norm_back(c)
        to_sibling(2, c)

    def run_down_weights(n):
        for i in range(NC):
            come(2, i)
        down_weights(n)

    def run_ffn_back(c):
        come(2, c)
        ffn_back(c)

    def run_first_back(c):
        cross_copy(2, c).wait_recv()
        first_norm_back(c)
        to_sibling(3, c)

    def run_attend_back(c):
        come(3, c)
        attend_back(c)

    def run_finish(c):
        cross_copy(3, c).wait_recv()
        finish(c)
        to_sibling(4, c)

    def run_results(_):
        for i in range(NC):
            come(1, i)

    def vector_copy():
        return remote(ns.vmine, ns.vsib, ns.pool_sem.at[2], ns.pool_sem.at[3], sib)

    def run_vectors(_):
        for i in range(7):
            ns.vmine[i : i + 1, :] = jnp.sum(ns.acc[i], axis=0, keepdims=True)
        ns.vmine[7:8, :] = jnp.zeros((1, D), F32)
        ns.vmine[7:8, 0:L] = jnp.sum(ns.acc[7], axis=0, keepdims=True)[:, :L]
        ns.vmine[7:8, 256 : 256 + L] = jnp.sum(ns.acc[8], axis=0, keepdims=True)[:, :L]
        vector_copy().start()

    def run_vectors_sum(_):
        vector_copy().wait()
        v = ns.vmine[...] + jnp.where(iota((8, D), 0) < 6, ns.vsib[...], 0.0)
        ns.vg[...] = jnp.concatenate([v[:, : D // 2], v[:, D // 2 :]], axis=0).astype(BF16)

    backward = (
        run_second_back, run_down_weights, run_ffn_back, lambda c: send_part(2, c, ffn_back_out),
        functools.partial(send_across, 2), up_weights, run_first_back, run_attend_back,
        lambda c: send_part(3, c, attend_back_out), functools.partial(send_across, 3), lambda _: attend_weights(),
        run_finish, functools.partial(come, 4), run_results, run_vectors, run_vectors_sum,
    )
    for k in z.order:
        if k in tasks:
            if k in z.free_before:
                ends_of.pop(z.free_before[k])()
            tasks[k]()
        elif k < VECTOR:
            backward[k // 10](k % 10)
    for end in ends_of.values():
        end()
    if not in_kernel:
        gsum[...] = grad[...]
        ns.vt[...] = ns.vg[...]
    for key in list(unsent):
        finish_send(key)
    for c in sends:
        c.wait_send()


def unpack_kernel(z, g, res_i, tg_i, vec, loss_i, gd, gu, res, tg, gq, gk, gv, go, *more):
    L, R, D = z.L, z.R, z.D
    ones, (bq, bv, loss, wide, sem) = more[:7], more[7:]
    stores = []

    def store(src, dst):
        stores.append(pltpu.make_async_copy(src, dst, sem.at[len(stores)]))
        stores[-1].start()

    rows = tg.shape[0] // 4
    for i in range(4):
        at = pl.ds(i * rows, rows)
        store(tg_i.at[at], tg.at[at])
    for m in range(3):
        for i, r in enumerate(range(0, D, L)):
            at = pl.ds(r, L)
            wide[m, at] = g[m, at].astype(F32)
            store(wide.at[m, at], (gq, gk, gv, go)[i] if m == 2 else (gd, gu)[m].at[at])
    for i in range(2):
        at = pl.ds(2 * i * rows, 2 * rows)
        store(res_i.at[at], res.at[at])
    v = vec[...].astype(F32)
    v = jnp.concatenate([v[:8], v[8:]], axis=1)
    for n, one in enumerate(ones):
        one[...] = v[n, :]
    bq[...] = v[7, 0:L]
    bv[...] = v[7, 256 : 256 + L]
    loss[...] = loss_i[0, 0 : R * 3]
    for c in stores:
        c.wait()


FORWARD = (
    0, 10, 20, 1, 11, 21, 12, 22, 13, 23, 30, 40, 50, 60, 41, 70, 51, 61, 42, 71, 52, 62, 43, 72, 53, 63, 73, 80, 81, 82, 83,
)
JOBS = (
    (0, 0, 32), (1, 0, 32), (3, 0, 80), (0, 0, 32), (0, 0, 96), (1, 0, 64), (0, 0, 96), (0, 0, 96), (1, 0, 64),
    (0, 0, 96), (3, 1, 80), (0, 1, 96), (1, 1, 96), (0, 1, 96), (0, 1, 96), (0, 1, 96), (1, 1, 64), (0, 1, 64),
    (0, 2, 96), (1, 2, 64), (0, 2, 96), (1, 2, 64), (0, 2, 96), (1, 2, 64), (0, 2, 96), (1, 2, 64), (0, 2, 64),
    (1, 2, 64),
)
VECTOR, JOB = 200, 1000
ORDER = (
    0, 1, 2, 3, 21, 10, 1010, 1000, 11, 1040, 1030, 1020, 12, 1070, 22, 1050, 31, 23, 20, 1080, 1060, 30, 1048,
    1011, 50, 51, 1110, 1021, 41, 1012, 1100, 1051, 40, 1013, 1130, 32, 1078, 1120, 52, 1081, 1068, 1041, 1071,
    42, 1052, 1022, 61, 1101, 1170, 1160, 1140, 1001, 33, 1053, 1121, 1082, 1061, 1178, 1014, 1141, 1150, 60,
    1102, 1042, 43, 1031, 70, 1072, 1090, 1138, 1054, 71, 1122, 1023, 1083, 1161, 1148, 1008, 1043, 1073, 1131,
    1062, 62, 1151, 1002, 1103, 80, 1091, 63, 1142, 1098, 1158, 1123, 1084, 72, 1162, 1132, 1063, 1118, 1024,
    73, 140, 1003, 90, 1143, 1152, 100, 82, 1190, 1104, 1092, 1111, 1124, 1163, 81, 1133, 150, 92, 1180, 1210,
    1220, 1025, 1240, 1004, 1074, 1144, 1191, 91, 1250, 1153, 83, 1093, 1015, 1038, 1105, 1055, 1026, 1164,
    130, 1171, 1145, 1032, 1260, 1211, 93, 1192, 200, 1112, 1154, 1181, 1064, 1200, 1106, 1075, 1033, 1230,
    1188, 1228, 110, 1270, 1085, 1251, 1134, 201, 1172, 1212, 1193, 1221, 1034, 1113, 1261, 120, 1044, 1182,
    1231, 112, 1201, 1173, 1213, 1174, 111, 1114, 1252, 1005, 1094, 121, 1271, 1194, 202, 1248, 1107, 1183,
    1268, 1035, 1241, 1222, 1184, 1095, 1224, 204, 1065, 1214, 1027, 1215, 1232, 1125, 1253, 1208, 1202, 203,
    1135, 1204, 113, 1272, 1264, 1262, 1244, 1223, 1185, 1242, 1233, 1155, 1115, 1175, 1255, 1203, 1045, 1263,
    123, 122, 1243, 1225, 1165, 1205, 1273, 1265, 1195, 1254, 1245, 1234, 1235, 1274, 1275,
)
G_SLOT = (0, 1, 0, 0, 2)
VMEM1 = 54 * 2**20


def send_slots(order, n_jobs):
    steps = [(n, k, (k - JOB) // 10) for n, k in enumerate(order) if k >= JOB]
    last = {i: n for n, _, i in steps}
    slots, free_before, done, used = {}, {}, [], 0
    for n, k, i in steps:
        if i not in slots:
            if done:
                old = done.pop(0)
                slots[i], free_before[k] = slots[old], old
            else:
                slots[i], used = used, used + 1
        if last[i] == n:
            done.append(i)
    return slots, free_before, used


def default_order(chunks):
    out = []
    for group in ((0,), (2, 3, 4)):
        out += [10 * k + c for c in range(chunks) for k in group]
    out += [130, 10, 11, 12, 50, 51, 52]
    for group in ((6,), (7,), (8, 9), (11, 12)):
        out += [10 * k + c for c in range(chunks) for k in group]
    return out + [100, 140, 150]


def on_device(n_dp, tokens, lengths, send_slot, recv_place, w_query, b_query, w_key, w_value, b_value, w_out,
              output_bias, first_norm_gain, first_norm_bias, w_up, b_up, w_down, down_bias, second_norm_gain,
              second_norm_bias, out_grad):
    T, D = tokens.shape
    R, L, F = lengths.shape[0], w_query.shape[1], w_up.shape[1]
    S, heads = T // R, L // HEAD_DIM
    QB = 256 if S % 256 == 0 else S
    n_qb, half = S // QB, QB // 2
    KW = min(QB + (MAX_PIECE if n_qb <= 2 else 2 * MAX_PIECE), S)
    NC = R * n_qb
    jobs, rx_at, rx_rows, at = [], [], 0, [0, 0, 0]
    for kind, j, n in JOBS:
        jobs.append((kind, j, at[j], n))
        rx_at.append(rx_rows)
        at[j] += 2 * n if kind == 3 else n
        rx_rows += n // 2 * 3 if kind == 0 else 2 * n
    n_jobs = len(jobs)
    slots, free_before, n_slots = send_slots(ORDER, n_jobs)
    order = ORDER if NC == 4 else default_order(NC)
    in_kernel = n_dp == 8 and at == [D, D, D] and NC == 4
    z = types.SimpleNamespace(n_dp=n_dp, R=R, S=S, D=D, L=L, F=F, heads=heads, in_kernel=in_kernel, QB=QB, KW=KW, TR=32,
                              unroll=4, jobs=jobs, rx_at=rx_at, order=order, slots=slots, free_before=free_before)
    ins = dict(lengths=lengths, send_slot=send_slot, recv_place=recv_place, b_query=b_query, b_value=b_value,
               output_bias=output_bias, first_norm_gain=first_norm_gain, first_norm_bias=first_norm_bias, b_up=b_up,
               down_bias=down_bias, second_norm_gain=second_norm_gain, second_norm_bias=second_norm_bias,
               tokens=tokens, wq=w_query.T, wk=w_key.T, wv=w_value.T, wo=w_out, wu=w_up, wd=w_down, og=out_grad)
    any_, vmem, smem = (pl.BlockSpec(memory_space=m) for m in (pl.ANY, pltpu.VMEM, pltpu.SMEM))
    in_specs = [smem] * 3 + [vmem] * 9 + [any_] * 8
    outs = dict(
        res=((T, D), BF16), tg=((T, D), F32), gsum=((3, D, D), BF16), vt=((16, D // 2), BF16), loss_v=((8, 128), F32)
    )
    V = pltpu.VMEM
    dma = pltpu.SemaphoreType.DMA
    scratch = dict(
        tokens_v=V((T, D), BF16), og_v=V((T, D), BF16), wq_v=V((L, D), BF16), wk_v=V((L, D), BF16),
        wv_v=V((L, D), BF16), wo_all=V((4, L, D), BF16), ctx_all=V((NC, 4, half, L), BF16), wu_v=V((D, F), BF16), wd_v=V((F, D), BF16), vecs=V((9, D), F32),
        q=V((T, L), BF16), k=V((T, L), BF16), v=V((T, L), BF16), ctx=V((T, L), BF16),
        dq=V((T, L), BF16), dk=V((T, L), BF16), dv=V((T, L), BF16), dk_acc=V((S, L), F32), dv_acc=V((S, L), F32),
        probs=V((NC * heads, QB, KW), BF16),
        xhat1=V((NC, half, D), F32), xhat2=V((NC, half, D), F32), hid=V((NC, half, D), F32), d2=V((NC, half, D), F32),
        d1=V((NC, half, D), F32), rstd1=V((NC, half, 1), F32), rstd2=V((NC, half, 1), F32),
        rest=V((half, D), BF16), dtok=V((half, D), F32),
        hl=V((T, D), BF16), act=V((T, F), BF16), gp=V((T, F), BF16), d2l=V((T, D), BF16), dup=V((T, F), BF16),
        d1l=V((T, D), BF16),
        part=V((2, NC, QB, D), BF16), arecv=V((2, NC, half, D), BF16),
        ysend=V((2, NC, half, D), BF16), yrecv=V((2, NC, half, D), BF16),
        pool=V((16, D), F32), pool_r=V((16, D), F32), dpool=V((16, D), F32), acc=V((9, 8, D), F32),
        outg=V((n_dp * 16, 128), BF16), inc=V((n_dp * 16, 128), BF16), outg2=V((n_dp * 16, 128), BF16),
        inc2=V((n_dp * 16, 128), BF16),
        vmine=V((8, D), F32), vsib=V((8, D), F32), vg=V((16, D // 2), BF16), vr=V((3, 16, D // 2), BF16),
        grad=V((3, D, D), BF16), rx=V((rx_rows, D), BF16),
        in_sem=dma((8,)), w_s=dma((3,)), w_r=dma((3,)), cx_s=dma((NC, 3)), cx_r=dma((NC, 3)), a_s=dma((2, NC)), a_r=dma((2, NC)), y_s=dma((2, NC)), y_r=dma((2, NC)),
        g_s=dma((5, NC)), g_r=dma((3, NC)), pool_sem=dma((4,)), p_s=dma((n_dp,)), p_r=dma((2, n_dp)),
        v_s=dma((2,)), v_r=dma((3,)), d_s=dma((n_slots, 2)), d_r=dma((n_jobs, 4)),
    )
    names = tuple(ins) + tuple(outs) + tuple(scratch)
    res, tg, grads, vec, loss = pl.pallas_call(
        functools.partial(layer_kernel, z, names),
        out_shape=[V(*s) for s in outs.values()],
        in_specs=in_specs,
        out_specs=[vmem] * 5,
        scratch_shapes=list(scratch.values()),
        compiler_params=pltpu.CompilerParams(
            collective_id=0, has_side_effects=True, vmem_limit_bytes=VMEM1
        ),
    )(*ins.values())
    if not z.in_kernel:
        grads, vec = lax.psum((grads, vec), "dp")
    un_outs = [((F, D), F32), ((D, F), F32), ((T, D), BF16), ((T, D), F32)] + [((L, D), F32)] * 4
    n_big = len(un_outs)
    un_outs += [((D,), F32)] * 7 + [((L,), F32)] * 2 + [((R * 3,), F32)]
    o = pl.pallas_call(
        functools.partial(unpack_kernel, z),
        out_shape=[jax.ShapeDtypeStruct(*s) for s in un_outs],
        in_specs=[vmem] * 5,
        out_specs=[any_] * n_big + [vmem] * (len(un_outs) - n_big),
        scratch_shapes=[V((3, D, D), F32), dma((6 + 3 * (D // L),))],
        compiler_params=pltpu.CompilerParams(vmem_limit_bytes=24 * 2**20),
    )(grads, res, tg, vec, loss)
    gd, gu, res, tg, gq, gk, gv, go, v0, v1, v2, v3, v4, v5, v6, bq, bv, loss = o
    return res, loss, tg, gq.T, bq, gk.T, gv.T, bv, go, v0, v1, v2, gu, v6, gd, v3, v4, v5


def solution(mesh):
    rows, flat, cut = P("dp", None), P("dp"), P("mp")
    across, down = P(None, "mp"), P("mp", None)
    return jax.shard_map(
        functools.partial(on_device, mesh.shape["dp"]),
        mesh=mesh,
        in_specs=(rows, rows, flat, flat, across, cut, across, across, cut, down, P(), P(), P(), across, cut, down,
                  P(), P(), P(), rows),
        out_specs=(rows, flat, rows, across, cut, across, across, cut, down, P(), P(), P(), across, cut, down, P(),
                   P(), P()),
        check_vma=False,
    )
```

```python
import functools
import types

import jax
import jax.numpy as jnp
from jax import lax
from jax.experimental import pallas as pl
from jax.experimental.pallas import tpu as pltpu
from jax.sharding import PartitionSpec as P

HEAD_DIM = 64
MAX_PIECE = 128
NEG_FILL = -1e30
NORM_EPS = 1e-12
UNIT_EPS = 1e-06
SIM_SCALE = 50.0
MESH = pl.DeviceIdType.MESH
F32, BF16, I32 = jnp.float32, jnp.bfloat16, jnp.int32
HIGHEST = lax.Precision.HIGHEST


def nn(a, b):
    return lax.dot_general(a, b, (((1,), (0,)), ((), ())), preferred_element_type=F32)


def nt(a, b):
    return lax.dot_general(a, b, (((1,), (1,)), ((), ())), preferred_element_type=F32)


def tn(a, b):
    return lax.dot_general(a, b, (((0,), (0,)), ((), ())), preferred_element_type=F32)


def iota(shape, axis):
    return lax.broadcasted_iota(I32, shape, axis)


def hi_lo(x):
    hi = x.astype(BF16).astype(F32)
    return hi, x - hi


def layer_kernel(z, names, *refs):
    ns = types.SimpleNamespace(**dict(zip(names, refs)))
    n_dp, R, S, D, L, F, heads = z.n_dp, z.R, z.S, z.D, z.L, z.F, z.heads
    QB, KW = z.QB, z.KW
    n_qb, half = S // QB, QB // 2
    NC = R * n_qb
    CH = D // 128
    dp, mp = lax.axis_index("dp"), lax.axis_index("mp")
    core = mp % 2
    other = 1 - core
    sib = (dp, mp + 1 - 2 * core)
    across = (dp, (mp + 2) % 4)
    diagonal = (dp, (mp + 3 - 2 * core) % 4)

    bar = pltpu.get_barrier_semaphore()
    for t in (sib, across, diagonal):
        pl.semaphore_signal(bar, inc=1, device_id=t, device_id_type=MESH)
    for d in range(1, n_dp):
        pl.semaphore_signal(bar, inc=1, device_id=((dp + d) % n_dp, mp), device_id_type=MESH)

    loads = []
    for i, (src, dst) in enumerate((
        (ns.wo, ns.wo_all.at[mp]), (ns.tokens, ns.tokens_v), (ns.wq, ns.wq_v), (ns.wk, ns.wk_v), (ns.wv, ns.wv_v),
        (ns.wu, ns.wu_v), (ns.wd, ns.wd_v), (ns.og, ns.og_v),
    )):
        loads.append(pltpu.make_async_copy(src, dst, ns.in_sem.at[i]))
        loads[-1].start()
    vecs = ns.vecs
    for i, x in enumerate((
        ns.b_query, ns.b_value, ns.output_bias, ns.first_norm_gain, ns.first_norm_bias, ns.b_up, ns.down_bias,
        ns.second_norm_gain, ns.second_norm_bias,
    )):
        n = x.shape[0]
        vecs[i : i + 1, 0:n] = x[...].reshape(1, n)
    pl.semaphore_wait(bar, 2 + n_dp)

    def remote(src, dst, ss, rs, to):
        ss = ns.s_pool.at[0] if ss is None else ss
        return pltpu.make_async_remote_copy(
            src_ref=src, dst_ref=dst, send_sem=ss, recv_sem=rs, device_id=to, device_id_type=MESH
        )

    def vec(i, n=None):
        return vecs[i : i + 1, : (n or D)]

    ends = []
    for r in range(R):
        total, row = 0, []
        for p in range(7):
            total = total + ns.lengths[r, p]
            row.append(total)
        ends.append(row)

    def seg_of(position, r):
        seg = jnp.zeros(position.shape, I32)
        for p in range(6):
            seg = seg + jnp.where(position >= ends[r][p], 1, 0)
        return seg

    lane_head = iota((1, L), 1) // HEAD_DIM

    def only_head(x, h):
        return jnp.where(lane_head == h, x, jnp.zeros_like(x))

    users, taken = [None] * z.pool, [0]

    def retire(i):
        condition, copy, _ = users[i]
        users[i] = None
        if condition is None:
            copy.wait_send()
        else:
            pl.when(condition)(copy.wait_send)

    def take():
        i = taken[0] % z.pool
        taken[0] += 1
        if users[i] is not None:
            retire(i)
        return i

    def begin_send(build, key=None):
        i = take()
        copy = build(ns.s_pool.at[i])
        copy.start()
        users[i] = (None, copy, key)

    def finish_send(key):
        for i, u in enumerate(users):
            if u is not None and u[2] == key:
                retire(i)

    def pair_copy(which, c, ss=None):
        par = which % 2
        return remote(ns.part.at[par, c, pl.ds(pl.multiple_of(other * half, half), half)], ns.arecv.at[par, c],
                      ss, ns.a_r.at[par, c], sib)

    def cross_copy(which, c, ss=None):
        par = which % 2
        return remote(ns.ysend.at[par, c], ns.yrecv.at[par, c], ss, ns.y_r.at[par, c], across)

    def send_part(which, c, compute):
        part = ns.part.at[which % 2, c]

        def put(cols, val):
            part[:, cols] = val.astype(BF16)

        if which >= 2:
            finish_send((0, which - 2, c))
        compute(c, put)
        begin_send(functools.partial(pair_copy, which, c), (0, which, c))

    def send_across(which, c):
        par = which % 2
        pair_copy(which, c).wait_recv()
        if which >= 2:
            finish_send((1, which - 2, c))
        own = pl.ds(pl.multiple_of(core * half, half), half)
        ns.ysend[par, c] = ns.part[par, c, own] + ns.arecv[par, c]
        begin_send(functools.partial(cross_copy, which, c), (1, which, c))

    def y_total(which, c, rows):
        par = which % 2
        return ns.ysend[par, c, rows].astype(F32) + ns.yrecv[par, c, rows].astype(F32)

    def at_chunk(c):
        return slice(c * QB, c * QB + QB)

    def halves(i, c, ss=None):
        rows = pl.ds(pl.multiple_of(c * QB + core * half, half), half)
        x = (ns.hl, ns.res, ns.d2l, ns.d1l, ns.tg)[i]
        return remote(x.at[rows], x.at[rows], ss, ns.g_r.at[G_SLOT[i], c], sib)

    def to_sibling(i, c):
        begin_send(functools.partial(halves, i, c))

    TR = z.TR

    def by_rows(fn):
        def body(i, _):
            fn(pl.ds(pl.multiple_of(i * TR, TR), TR), i * TR)
            return 0

        lax.fori_loop(0, half // TR, body, 0, unroll=z.unroll)

    def fold(x):
        return jnp.sum(x.reshape(x.shape[0] // 8, 8, x.shape[1]), axis=0)

    def row_ds(c, start, n):
        return pl.ds(pl.multiple_of(c * QB + core * half + start, n), n)

    def columns(width, step=256):
        return [slice(n, n + step) for n in range(0, width, step)]

    def project(r):
        rows = pl.ds(r * S, S)
        x = ns.tokens_v[rows, :]
        ns.q[rows, :] = ((nt(x, ns.wq_v[...]) + vec(0, L)).astype(BF16) * (HEAD_DIM**-0.5)).astype(BF16)
        ns.k[rows, :] = nt(x, ns.wk_v[...]).astype(BF16)
        ns.v[rows, :] = (nt(x, ns.wv_v[...]) + vec(1, L)).astype(BF16)

    def win(b):
        return min(max(b * QB - MAX_PIECE, 0), S - KW)

    def attend(c):
        r, b = c // n_qb, c % n_qb
        q0, k0 = c * QB, r * S + win(b)
        same = seg_of(iota((QB, 1), 0) + b * QB, r) == seg_of(iota((1, KW), 1) + win(b), r)
        qb = ns.q[q0 : q0 + QB, :]
        kb = ns.k[k0 : k0 + KW, :]
        vb = ns.v[k0 : k0 + KW, :]
        ctx = None
        for h in range(heads):
            s = jnp.where(same, nt(only_head(qb, h), kb), NEG_FILL)
            e = jnp.exp(s - jnp.max(s, axis=-1, keepdims=True))
            p = (e * (1.0 / jnp.sum(e, axis=-1, keepdims=True))).astype(BF16)
            ns.probs[c * heads + h] = p
            o = nn(p, only_head(vb, h))
            ctx = o if ctx is None else ctx + o
        ns.ctx[q0 : q0 + QB, :] = ctx.astype(BF16)

    def weight_copy(k, ss=None):
        if k == 2:
            x = ns.wo_all.at[(mp + 2) % 4]
        else:
            x = ns.wo_all.at[mp]
        return remote(x, x, ss, ns.w_r.at[k], (sib, across, sib)[k])

    def context_copy(c, k, ss=None):
        mine = k == 1
        rows = pl.ds(pl.multiple_of(c * QB + (core if mine else other) * half, half), half)
        return remote(ns.ctx.at[rows], ns.ctx_all.at[c, mp], ss, ns.cx_r.at[c, k], (sib, across, diagonal)[k])

    def send_context(c):
        for k in (1, 2, 0):
            begin_send(functools.partial(context_copy, c, k))
        ns.ctx_all[c, mp] = ns.ctx[row_ds(c, 0, half), :]

    def attn_out(c):
        for w in columns(D):
            total = nn(ns.ctx_all[c, 0], ns.wo_all[0, :, w])
            for k in range(1, 4):
                total = total + nn(ns.ctx_all[c, k], ns.wo_all[k, :, w])
            ns.dtok[:, w] = total

    def norm(v):
        mean = jnp.mean(v, axis=-1, keepdims=True)
        d = v - mean
        rstd = lax.rsqrt(jnp.mean(d * d, axis=-1, keepdims=True) + NORM_EPS)
        return d * rstd, rstd

    def first_norm(c):
        def body(rows, start):
            mine = row_ds(c, start, TR)
            xh, rstd = norm(ns.tokens_v[mine].astype(F32) + ns.dtok[rows] + vec(2))
            ns.xhat1[c, rows] = xh
            ns.rstd1[c, rows] = rstd
            h = xh * vec(3) + vec(4)
            ns.hid[c, rows] = h
            ns.hl[mine] = h.astype(BF16)

        by_rows(body)

    def ffn_up(c):
        x = ns.hl[at_chunk(c), :]
        for w in columns(F):
            u = nn(x, ns.wu_v[:, w]) + vecs[5:6, w]
            phi = 0.5 + 0.5 * lax.erf(u * 0.7071067811865476)
            ns.act[at_chunk(c), w] = (u * phi).astype(BF16)
            ns.gp[at_chunk(c), w] = (phi + u * (jnp.exp(-0.5 * (u * u)) * 0.3989422804014327)).astype(BF16)

    def ffn_down(c, put):
        x = ns.act[at_chunk(c), :]
        for w in columns(D):
            put(w, nn(x, ns.wd_v[:, w]))

    def second_norm(c):
        r, b = c // n_qb, c % n_qb

        def body(rows, start):
            xh, rstd = norm(ns.hid[c, rows] + y_total(1, c, rows) + vec(6))
            ns.xhat2[c, rows] = xh
            ns.rstd2[c, rows] = rstd
            res = xh * vec(7) + vec(8)
            low = res.astype(BF16)
            ns.res[row_ds(c, start, TR)] = low
            ns.rest[rows] = (res - low.astype(F32)).astype(BF16)

        by_rows(body)
        piece = iota((8, half), 0)
        seg = seg_of(iota((8, half), 1) + (core * half + b * QB), r)
        member = jnp.where((seg == piece) & (piece < 6), 1.0, 0.0).astype(BF16)
        at = slice(r * 8, r * 8 + 8)
        ns.pool[at, :] += nn(member, ns.res[row_ds(c, 0, half)]) + nn(member, ns.rest[...])

    PR = 16
    n_sent = R * 6

    def per_row(values, axis, shape, fill):
        pos = iota(shape, axis) % PR
        out = jnp.full(shape, fill, I32)
        for s in range(n_sent):
            out = jnp.where(pos == (s // 6) * 8 + s % 6, values[s], out)
        return out

    def slot_onehot(axis):
        shape = (n_dp * 16, CH * PR) if axis == 1 else (CH * PR, n_dp * 16)
        line = (1, CH * PR) if axis == 1 else (CH * PR, 1)
        vals = [ns.send_slot[s] // 2 * 16 + ns.send_slot[s] % 2 for s in range(n_sent)]
        target = per_row(vals, axis if axis == 1 else 0, line, -65536) + iota(line, 1 if axis == 1 else 0) // PR * 2
        return jnp.where(iota(shape, 0 if axis == 1 else 1) == target, 1.0, 0.0).astype(BF16)

    def place_onehot(axis):
        line = (1, n_dp * 16) if axis == 1 else (n_dp * 16, 1)
        shape = (CH * PR, n_dp * 16) if axis == 1 else (n_dp * 16, CH * PR)
        pos = iota(line, axis)
        slot = pos // 16 * 2 + pos % 2
        target = jnp.zeros(line, I32)
        for s in range(2 * n_dp):
            target = jnp.where(slot == s, ns.recv_place[s], target)
        target = target + pos % 16 // 2 * PR
        return jnp.where(iota(shape, 0 if axis == 1 else 1) == target, 1.0, 0.0).astype(BF16)

    def stack(x):
        return jnp.concatenate([x[:, c * 128 : c * 128 + 128] for c in range(CH)], axis=0)

    def unstack(x):
        return jnp.concatenate([x[c * PR : c * PR + PR] for c in range(CH)], axis=1)

    def peers(src, dst, rsem):
        mine = pl.ds(pl.multiple_of(dp * 16, 16), 16)

        def copy(d, ss=None):
            t = (dp + d) % n_dp
            return remote(src.at[pl.ds(pl.multiple_of(t * 16, 16), 16)], dst.at[mine], ss, rsem.at[d], (t, mp))

        for d in range(1, n_dp):
            begin_send(functools.partial(copy, d))
        dst[mine] = src[mine]
        for d in range(1, n_dp):
            copy(d).wait_recv()

    def pairs():
        begin_send(lambda ss: remote(ns.pool, ns.pool_r, ss, ns.pool_sem.at[0], sib))
        lens = [ns.lengths[s // 6, s % 6] for s in range(n_sent)]
        size = per_row(lens, 0, (PR, 1), 1).astype(F32)
        inv = 1.0 / size
        hot = slot_onehot(1)
        remote(ns.pool, ns.pool_r, None, ns.pool_sem.at[0], sib).wait_recv()
        pooled = (ns.pool[...] + ns.pool_r[...]) * inv
        ns.outg[...] = nn(hot, stack(pooled).astype(BF16)).astype(BF16)
        peers(ns.outg, ns.inc, ns.p_r.at[0])
        o = unstack(nn(place_onehot(1), ns.inc[...]))
        s = lax.rsqrt(jnp.sum(o * o, axis=-1, keepdims=True) + UNIT_EPS)
        u = o * s
        logits = SIM_SCALE * lax.dot_general(
            u, u, (((1,), (1,)), ((), ())), precision=HIGHEST, preferred_element_type=F32
        )
        i, j = iota((PR, PR), 0), iota((PR, PR), 1)
        live = (i % 2 == 0) & (i < n_sent) & (j % 2 == 1) & (j < n_sent)
        lm = jnp.where(live, logits, NEG_FILL)
        peak = jnp.max(lm, axis=-1, keepdims=True)
        e = jnp.where(live, jnp.exp(lm - peak), 0.0)
        tot = jnp.maximum(jnp.sum(e, axis=-1, keepdims=True), 1e-30)
        partner = live & (j == i + 1)
        loss = peak + jnp.log(tot) - jnp.sum(jnp.where(partner, logits, 0.0), axis=-1, keepdims=True)
        i2, j2 = iota((PR, 128), 0), iota((PR, 128), 1)
        ns.loss_v[...] = jnp.broadcast_to(
            jnp.sum(jnp.where((i2 == 2 * j2) & (i2 < n_sent), loss, 0.0), axis=0, keepdims=True), (8, 128)
        )
        dl = e / tot - jnp.where(partner, 1.0, 0.0)
        du = SIM_SCALE * (
            lax.dot_general(dl, u, (((1,), (0,)), ((), ())), precision=HIGHEST, preferred_element_type=F32)
            + lax.dot_general(dl, u, (((0,), (0,)), ((), ())), precision=HIGHEST, preferred_element_type=F32)
        )
        do = s * (du - u * jnp.sum(u * du, axis=-1, keepdims=True))
        ns.outg2[...] = nn(place_onehot(0), stack(do).astype(BF16)).astype(BF16)
        peers(ns.outg2, ns.inc2, ns.p_r.at[1])
        ns.dpool[...] = unstack(nn(slot_onehot(0), ns.inc2[...])) * inv

    def norm_back(dx, xh, rstd):
        return rstd * (
            dx - jnp.mean(dx, axis=-1, keepdims=True) - xh * jnp.mean(dx * xh, axis=-1, keepdims=True)
        )

    def second_norm_back(c):
        r, b = c // n_qb, c % n_qb
        hi, lo = hi_lo(ns.dpool[r * 8 : r * 8 + 8, :])
        lane = iota((half, 16), 1) % 8
        seg = seg_of(iota((half, 1), 0) + (core * half + b * QB), r)
        member = jnp.where((seg == lane) & (lane < 6), 1.0, 0.0).astype(BF16)
        ns.dtok[...] = nn(member, jnp.concatenate([hi, lo], axis=0).astype(BF16))

        def body(rows, start):
            mine = row_ds(c, start, TR)
            d = ns.og_v[mine].astype(F32) + ns.dtok[rows]
            xh = ns.xhat2[c, rows]
            ns.acc[4] += fold(d * xh)
            ns.acc[5] += fold(d)
            d2 = norm_back(d * vec(7), xh, ns.rstd2[c, rows])
            ns.acc[3] += fold(d2)
            ns.d2[c, rows] = d2
            ns.d2l[mine] = d2.astype(BF16)

        by_rows(body)

    def ffn_back(c):
        rows = at_chunk(c)
        x = ns.d2l[rows, :]
        for w in columns(F):
            da = nt(x, ns.wd_v[w, :]).astype(BF16)
            du = (da.astype(F32) * ns.gp[rows, w].astype(F32)).astype(BF16)
            ns.dup[rows, w] = du
            ns.acc[6, :, w] += fold(du.astype(F32))

    def ffn_back_out(c, put):
        x = ns.dup[at_chunk(c), :]
        for w in columns(D):
            put(w, nt(x, ns.wu_v[w, :]))

    def down_weights(n):
        for w in columns(F)[n : n + 1]:
            grad[0, w, :] = tn(ns.act[:, w], ns.d2l[...]).astype(BF16)

    def up_weights(n):
        for w in columns(D)[n : n + 1]:
            grad[1, w, :] = tn(ns.hl[:, w], ns.dup[...]).astype(BF16)

    def first_norm_back(c):
        def body(rows, start):
            mine = row_ds(c, start, TR)
            d = ns.d2[c, rows] + y_total(2, c, rows)
            xh = ns.xhat1[c, rows]
            ns.acc[1] += fold(d * xh)
            ns.acc[2] += fold(d)
            d1 = norm_back(d * vec(3), xh, ns.rstd1[c, rows])
            ns.acc[0] += fold(d1)
            ns.d1[c, rows] = d1
            ns.d1l[mine] = d1.astype(BF16)

        by_rows(body)

    def attend_back(c):
        r, b = c // n_qb, c % n_qb
        q0, k0 = c * QB, r * S + win(b)
        cb = nt(ns.d1l[at_chunk(c), :], ns.wo_all[mp]).astype(BF16)
        qb = ns.q[q0 : q0 + QB, :]
        kb = ns.k[k0 : k0 + KW, :]
        vb = ns.v[k0 : k0 + KW, :]
        dq = dk = dv = None
        for h in range(heads):
            p = ns.probs[c * heads + h]
            dp_ = nt(cb, only_head(vb, h))
            pf = p.astype(F32)
            delta = jnp.sum(pf * dp_, axis=-1, keepdims=True)
            ds = (pf * (dp_ - delta)).astype(BF16)
            t, u, w = nn(ds, only_head(kb, h)), tn(ds, only_head(qb, h)), tn(p, only_head(cb, h))
            dq, dk, dv = (t, u, w) if dq is None else (dq + t, dk + u, dv + w)
        dq = (dq * (HEAD_DIM**-0.5)).astype(BF16)
        ns.dq[q0 : q0 + QB, :] = dq
        ns.acc[7, :, :L] += fold(dq.astype(F32))
        at = slice(win(b), win(b) + KW)
        if b == 0:
            ns.dk_acc[r] = jnp.zeros((S, L), F32)
            ns.dv_acc[r] = jnp.zeros((S, L), F32)
        ns.dk_acc[r, at, :] += dk
        ns.dv_acc[r, at, :] += dv
        if b == n_qb - 1:
            rows = slice(r * S, r * S + S)
            ns.dk[rows, :] = ns.dk_acc[r].astype(BF16)
            dvr = ns.dv_acc[r].astype(BF16)
            ns.dv[rows, :] = dvr
            ns.acc[8, :, :L] += fold(dvr.astype(F32))

    def attend_back_out(c, put):
        at = at_chunk(c)
        for w in columns(D):
            put(
                w,
                nn(ns.dq[at, :], ns.wq_v[:, w])
                + nn(ns.dk[at, :], ns.wk_v[:, w])
                + nn(ns.dv[at, :], ns.wv_v[:, w]),
            )

    def attend_weights():
        for i, x in enumerate((ns.dq, ns.dk, ns.dv)):
            grad[2, i * L : i * L + L, :] = tn(x[...], ns.tokens_v[...]).astype(BF16)
        grad[2, 3 * L : 4 * L, :] = tn(ns.ctx[...], ns.d1l[...]).astype(BF16)

    def finish(c):
        def body(rows, start):
            ns.tg[row_ds(c, start, TR)] = ns.d1[c, rows] + y_total(3, c, rows)

        by_rows(body)

    xi, zi = dp % 2, dp // 2
    nz = n_dp // 2
    in_kernel = z.in_kernel
    outer = (zi == 0) | (zi == nz - 1)
    inner = (zi != 0) & (zi != nz - 1)
    xp = (dp + 1 - 2 * xi, mp)
    zp = (dp + 2 - 4 * (zi % 2), mp)
    zq = ((dp + 2 * (3 - 2 * zi)) % n_dp if in_kernel else dp, mp)
    ii = zi // 2
    grad, gsum = ns.grad, ns.gsum

    def when(condition, fn):
        return lambda: pl.when(condition)(fn)

    def add_into(dst, dst_at, a_at, b_at, n):
        step = 48 if n % 48 == 0 else 32 if n % 32 == 0 else 16

        def body(i, _):
            o = i * step
            x = grad[a_at[0], pl.ds(pl.multiple_of(a_at[1] + o, 16), step), :]
            y = ns.rx[pl.ds(pl.multiple_of(b_at + o, 16), step), :]
            dst[dst_at[0], pl.ds(pl.multiple_of(dst_at[1] + o, 16), step), :] = x + y
            return 0

        lax.fori_loop(0, n // step, body, 0)

    def step(condition, first, *builds):
        def run():
            at = [take() for _ in builds]

            def body():
                first()
                for i, build in zip(at, builds):
                    build(ns.s_pool.at[i]).start()

            if condition is None:
                body()
            else:
                pl.when(condition)(body)
            for i, build in zip(at, builds):
                users[i] = (condition, build(ns.s_pool.at[i]), None)

        return run

    def nothing():
        pass

    def copies(slot, *all_of):
        return [
            functools.partial(lambda src, dst, k, to, ss=None: remote(src, dst, ss, ns.d_r.at[slot, k], to), *one)
            for one in all_of
        ]

    def got(*builds):
        def first():
            for build in builds:
                build().wait_recv()

        return first

    def got_add(build, dst, row, at, n):
        def first():
            build().wait_recv()
            add_into(dst, row, row, at, n)

        return first

    def x_job(slot, j, r0, n):
        h = n // 2
        mine = pl.multiple_of(r0 + xi * h, 16)
        yours = pl.multiple_of(r0 + (1 - xi) * h, 16)
        own, theirs = grad.at[j, pl.ds(mine, h)], grad.at[j, pl.ds(yours, h)]
        done = gsum.at[j, pl.ds(mine, h)]
        b0 = z.rx_at[slot]
        buf = lambda k: ns.rx.at[pl.ds(b0 + k * h, h)]
        x1, z1, z2, z3, x2 = copies(
            slot, (theirs, buf(0), 0, xp), (own, buf(1), 1, zp), (own, buf(2), 2, zq), (done, done, 1, zp), (done, done, 3, xp)
        )
        return {
            0: step(None, nothing, x1),
            1: step(outer, got_add(x1, grad, (j, mine), b0, h), z1),
            8: step(inner, got_add(x1, grad, (j, mine), b0, h)),
            2: step(inner, got_add(z1, grad, (j, mine), b0 + h, h), z2),
            3: step(inner, got_add(z2, gsum, (j, mine), b0 + 2 * h, h), z3, x2),
            4: step(outer, got(z3), x2),
            5: step(None, got(x2)),
        }

    def z_job(slot, j, r0, n, quarters=False):
        h, f = n // 2, n // 4
        mine = pl.multiple_of(r0 + ii * h, 16)
        yours = pl.multiple_of(r0 + (1 - ii) * h, 16)
        own, theirs, whole = grad.at[j, pl.ds(mine, h)], grad.at[j, pl.ds(yours, h)], grad.at[j, pl.ds(r0, n)]
        done, done_b = gsum.at[j, pl.ds(mine, h)], gsum.at[j, pl.ds(yours, h)]
        back_a, back_b = done, done_b
        if quarters:
            back_a = gsum.at[j, pl.ds(pl.multiple_of(mine + xi * f, 16), f)]
            back_b = gsum.at[j, pl.ds(pl.multiple_of(yours + xi * f, 16), f)]
        b0 = z.rx_at[slot]
        buf = lambda k: ns.rx.at[pl.ds(b0 + k * h, h)]
        z1, z2, x, z2b, z3a, z3b, xa, xb = copies(
            slot, (whole, ns.rx.at[pl.ds(b0 + n, n)], 0, zp), (theirs, buf(0), 1, zq), (own, buf(1), 2, xp),
            (done, done, 3, zq), (back_a, back_a, 0, zp), (back_b, back_b, 1, zp), (back_a, back_a, 2, xp),
            (back_b, back_b, 3, xp),
        )
        steps = {
            0: step(outer, nothing, z1),
            1: step(inner, got_add(z1, grad, (j, r0), b0 + n, n), z2),
            2: step(inner, got_add(z2, grad, (j, mine), b0, h), x),
            3: step(inner, got_add(x, gsum, (j, mine), b0 + h, h), z2b, z3a),
            4: step(inner, got(z2b), z3b),
        }
        if quarters:
            steps[5] = step(outer, got(z3a, z3b), xa, xb)
            steps[6] = step(outer, got(xa, xb))
        else:
            steps[5] = step(outer, got(z3a, z3b))
        return steps

    def u_job(slot, j, r0, n):
        near = pl.multiple_of(r0 + ii * n, 16)
        far = pl.multiple_of(r0 + (1 - ii) * n, 16)
        near_g, far_g = grad.at[j, pl.ds(near, n)], grad.at[j, pl.ds(far, n)]
        near_s, far_s = gsum.at[j, pl.ds(near, n)], gsum.at[j, pl.ds(far, n)]
        b0 = z.rx_at[slot]
        buf = lambda k: ns.rx.at[pl.ds(b0 + k * n, n)]
        za, ma, zb, xa, zc, mb, zd = copies(
            slot, (far_g, buf(0), 0, zp), (far_g, buf(1), 1, zq), (near_g, buf(0), 0, zp), (near_g, buf(1), 1, xp),
            (near_s, near_s, 2, zp), (near_s, near_s, 3, zq), (far_s, far_s, 2, zp),
        )
        return {
            0: step(outer, nothing, za),
            1: step(inner, got_add(za, grad, (j, far), b0, n), ma),
            2: step(inner, got_add(ma, grad, (j, near), b0 + n, n), zb),
            3: step(outer, got_add(zb, grad, (j, near), b0, n), xa),
            4: step(outer, got_add(xa, gsum, (j, near), b0 + n, n), zc),
            5: step(inner, got(zc), mb),
            6: step(inner, got(mb), zd),
            7: step(outer, got(zd)),
        }

    def vector_job():
        vg, vr = ns.vg, ns.vr
        s = lambda k: ns.v_s.at[k]
        q = lambda k: ns.v_r.at[k]
        z1 = remote(vg, vr.at[0], s(0), q(0), zp)
        z2 = remote(vg, vr.at[1], s(0), q(1), zq)
        x = remote(vg, vr.at[2], s(1), q(2), xp)
        z3 = remote(ns.vt, ns.vt, s(0), q(0), zp)

        def c1():
            z1.wait_recv()
            vg[...] = vg[...] + vr[0]
            z2.start()

        def c2():
            z2.wait_recv()
            z2.wait_send()
            vg[...] = vg[...] + vr[1]
            x.start()

        def c3():
            x.wait_recv()
            ns.vt[...] = vg[...] + vr[2]
            z3.start()

        def end():
            pl.when(outer)(z1.wait_send)

            @pl.when(inner)
            def _():
                x.wait_send()
                z3.wait_send()

        steps = {0: when(outer, z1.start), 1: when(inner, c1), 2: when(inner, c2), 3: when(inner, c3),
                 4: when(outer, z3.wait_recv)}
        return steps, end

    tasks, ends_of = {}, {}
    if in_kernel:
        for i, (kind, j, r0, n) in enumerate(z.jobs):
            job = (x_job, z_job, functools.partial(z_job, quarters=True), u_job)[kind]
            tasks.update({JOB + i * 10 + k: f for k, f in job(i, j, r0, n).items()})
        steps, end = vector_job()
        tasks.update({VECTOR + k: f for k, f in steps.items()})
        ends_of[-1] = end

    waited = set()

    def once(key, fn):
        if key not in waited:
            waited.add(key)
            fn()

    def load(*keys):
        for k in keys:
            once((9, k), loads[k].wait)

    def come(i, c):
        once((i, c), halves(i, c).wait_recv)

    load(0)
    for k in (1, 0):
        begin_send(functools.partial(weight_copy, k))
    ns.pool[...] = jnp.zeros((PR, D), F32)
    ns.acc[...] = jnp.zeros(ns.acc.shape, F32)

    def run_project(r):
        load(1, 2, 3, 4)
        project(r)

    def run_relay(_):
        weight_copy(1).wait_recv()
        begin_send(functools.partial(weight_copy, 2))

    def run_norm(c):
        for k in range(3):
            context_copy(c, k).wait_recv()
        for k in (0, 2):
            once((8, k), weight_copy(k).wait_recv)
        attn_out(c)
        first_norm(c)
        to_sibling(0, c)

    def run_up(c):
        load(5)
        come(0, c)
        ffn_up(c)

    def run_down(c):
        load(6)
        send_part(1, c, ffn_down)

    def run_second(c):
        cross_copy(1, c).wait_recv()
        second_norm(c)
        to_sibling(1, c)

    forward = (run_project, attend, send_context, run_relay, run_norm, run_up, run_down,
               functools.partial(send_across, 1), run_second)
    if NC == 4:
        plan = FORWARD
    else:
        plan = [r for r in range(R)]
        plan += [10 * k + c for c in range(NC) for k in (1, 2)] + [30]
        for group in ((4, 5, 6, 7), (8,)):
            plan += [10 * k + c for c in range(NC) for k in group]
    for k in plan:
        forward[k // 10](k % 10)
    load(7)
    pairs()

    def run_second_back(c):
        second_norm_back(c)
        to_sibling(2, c)

    def run_down_weights(n):
        for i in range(NC):
            come(2, i)
        down_weights(n)

    def run_ffn_back(c):
        come(2, c)
        ffn_back(c)

    def run_first_back(c):
        cross_copy(2, c).wait_recv()
        first_norm_back(c)
        to_sibling(3, c)

    def run_attend_back(c):
        come(3, c)
        attend_back(c)

    def run_finish(c):
        cross_copy(3, c).wait_recv()
        finish(c)
        to_sibling(4, c)

    def run_results(_):
        for i in range(NC):
            come(1, i)

    def vector_copy(ss=None):
        return remote(ns.vmine, ns.vsib, ss, ns.pool_sem.at[1], sib)

    def run_vectors(_):
        for i in range(7):
            ns.vmine[i : i + 1, :] = jnp.sum(ns.acc[i], axis=0, keepdims=True)
        ns.vmine[7:8, :] = jnp.zeros((1, D), F32)
        ns.vmine[7:8, 0:L] = jnp.sum(ns.acc[7], axis=0, keepdims=True)[:, :L]
        ns.vmine[7:8, 256 : 256 + L] = jnp.sum(ns.acc[8], axis=0, keepdims=True)[:, :L]
        begin_send(vector_copy)

    def run_vectors_sum(_):
        vector_copy().wait_recv()
        v = ns.vmine[...] + jnp.where(iota((8, D), 0) < 6, ns.vsib[...], 0.0)
        ns.vg[...] = jnp.concatenate([v[:, : D // 2], v[:, D // 2 :]], axis=0).astype(BF16)

    backward = (
        run_second_back, run_down_weights, run_ffn_back, lambda c: send_part(2, c, ffn_back_out),
        functools.partial(send_across, 2), up_weights, run_first_back, run_attend_back,
        lambda c: send_part(3, c, attend_back_out), functools.partial(send_across, 3), lambda _: attend_weights(),
        run_finish, functools.partial(come, 4), run_results, run_vectors, run_vectors_sum,
    )
    for k in z.order:
        if k in tasks:
            tasks[k]()
        elif k < VECTOR:
            backward[k // 10](k % 10)
    for end in ends_of.values():
        end()
    if not in_kernel:
        gsum[...] = grad[...]
        ns.vt[...] = ns.vg[...]
    for i, u in enumerate(users):
        if u is not None:
            retire(i)


def unpack_kernel(z, g, res_i, tg_i, vec, loss_i, gd, gu, res, tg, gq, gk, gv, go, *more):
    L, R, D = z.L, z.R, z.D
    ones, (bq, bv, loss, wide, sem) = more[:7], more[7:]
    stores = []

    def store(src, dst):
        stores.append(pltpu.make_async_copy(src, dst, sem.at[len(stores)]))
        stores[-1].start()

    rows = tg.shape[0] // 4
    for i in range(4):
        at = pl.ds(i * rows, rows)
        store(tg_i.at[at], tg.at[at])
    for m in range(3):
        for i, r in enumerate(range(0, D, L)):
            at = pl.ds(r, L)
            wide[m, at] = g[m, at].astype(F32)
            store(wide.at[m, at], (gq, gk, gv, go)[i] if m == 2 else (gd, gu)[m].at[at])
    for i in range(2):
        at = pl.ds(2 * i * rows, 2 * rows)
        store(res_i.at[at], res.at[at])
    v = vec[...].astype(F32)
    v = jnp.concatenate([v[:8], v[8:]], axis=1)
    for n, one in enumerate(ones):
        one[...] = v[n, :]
    bq[...] = v[7, 0:L]
    bv[...] = v[7, 256 : 256 + L]
    loss[...] = loss_i[0, 0 : R * 3]
    for c in stores:
        c.wait()


FORWARD = (
    0, 10, 20, 1, 11, 21, 12, 22, 13, 23, 30, 40, 50, 60, 41, 70, 51, 61, 42, 71, 52, 62, 43, 72, 53, 63, 73, 80, 81, 82, 83,
)
JOBS = (
    (3, 0, 48), (0, 0, 128), (3, 0, 32), (0, 0, 96), (0, 0, 96), (0, 0, 96), (2, 0, 64), (1, 0, 32),
    (0, 0, 32), (0, 0, 32), (0, 0, 32), (0, 1, 96), (3, 1, 32), (0, 1, 32), (0, 1, 96), (1, 1, 96), (0, 1, 32),
    (0, 1, 128), (1, 1, 32), (0, 1, 32), (0, 1, 32), (0, 1, 32), (2, 1, 64), (0, 1, 32), (0, 2, 96),
    (3, 2, 32), (0, 2, 96), (3, 2, 32), (0, 2, 96), (0, 2, 96), (0, 2, 64), (2, 2, 128), (0, 2, 64),
)
VECTOR, JOB = 200, 1000
ORDER = (
    0, 1, 2, 3, 21, 10, 1000, 1010, 11, 1030, 31, 1020, 22, 12, 1060, 41, 1090, 32, 1050, 23, 1001, 20, 1011,
    50, 1021, 1120, 1080, 30, 1110, 51, 40, 1100, 1160, 52, 1210, 1031, 1170, 1061, 42, 1220, 1002, 1200, 1018,
    33, 1121, 1130, 1091, 1098, 1051, 1062, 1101, 1012, 1118, 1038, 1022, 1140, 1032, 60, 1190, 1230, 1092,
    1221, 61, 1058, 1013, 1208, 1063, 1023, 1052, 43, 1108, 1040, 1218, 1211, 1171, 1150, 1168, 70, 1178, 1033,
    1122, 1003, 1212, 1093, 1161, 1102, 62, 71, 1172, 1088, 1222, 1238, 1201, 1014, 1111, 1064, 72, 1213, 130,
    1053, 1024, 1151, 1202, 1231, 1162, 1034, 80, 1112, 1103, 1180, 1148, 1223, 63, 1141, 1048, 1094, 1065,
    1152, 1173, 1025, 1123, 1232, 73, 1113, 1203, 1054, 1181, 1041, 1142, 1138, 100, 1290, 1224, 1153, 1042,
    1250, 140, 83, 1320, 1124, 1026, 1182, 1260, 90, 1143, 1251, 1271, 1280, 1154, 1104, 81, 1270, 91, 150,
    1298, 1292, 1191, 201, 1328, 200, 1240, 1174, 1291, 1163, 1131, 93, 1198, 1310, 1125, 1252, 1261, 1144,
    1233, 1132, 1183, 1204, 1268, 1114, 1300, 1081, 1253, 1192, 1272, 1321, 202, 1293, 1281, 1311, 1115, 1273,
    1164, 1035, 1015, 1225, 1043, 1234, 1070, 1241, 1082, 1262, 1294, 1288, 1301, 1184, 1322, 1127, 1126, 82,
    1254, 1312, 1133, 1134, 1193, 1194, 1248, 1214, 1027, 111, 1044, 1084, 1274, 203, 1308, 1083, 110, 1282,
    1155, 1263, 1066, 1071, 1055, 1323, 1165, 1004, 1242, 1264, 1185, 1302, 92, 1283, 1324, 1072, 1313, 1295,
    1243, 1255, 1275, 1284, 121, 1244, 1304, 1135, 1215, 1095, 1315, 1303, 1314, 1005, 113, 1256, 204, 1276,
    1085, 112, 1073, 1045, 1006, 1325, 1007, 1145, 122, 1277, 1245, 1205, 1105, 120, 123, 1235, 1285, 1305,
    1195, 1265, 1257, 1175, 1316, 1226, 1074, 1075,
)
G_SLOT = (0, 1, 0, 0, 2)
VMEM1 = 54 * 2**20
POOL = 48


def default_order(chunks):
    out = []
    for group in ((0,), (2, 3, 4)):
        out += [10 * k + c for c in range(chunks) for k in group]
    out += [130, 10, 11, 12, 50, 51, 52]
    for group in ((6,), (7,), (8, 9), (11, 12)):
        out += [10 * k + c for c in range(chunks) for k in group]
    return out + [100, 140, 150]


def on_device(n_dp, tokens, lengths, send_slot, recv_place, w_query, b_query, w_key, w_value, b_value, w_out,
              output_bias, first_norm_gain, first_norm_bias, w_up, b_up, w_down, down_bias, second_norm_gain,
              second_norm_bias, out_grad):
    T, D = tokens.shape
    R, L, F = lengths.shape[0], w_query.shape[1], w_up.shape[1]
    S, heads = T // R, L // HEAD_DIM
    QB = 256 if S % 256 == 0 else S
    n_qb, half = S // QB, QB // 2
    KW = min(QB + (MAX_PIECE if n_qb <= 2 else 2 * MAX_PIECE), S)
    NC = R * n_qb
    jobs, rx_at, rx_rows, at = [], [], 0, [0, 0, 0]
    for kind, j, n in JOBS:
        jobs.append((kind, j, at[j], n))
        rx_at.append(rx_rows)
        at[j] += 2 * n if kind == 3 else n
        rx_rows += n // 2 * 3 if kind == 0 else 2 * n
    n_jobs = len(jobs)
    order = ORDER if NC == 4 else default_order(NC)
    in_kernel = n_dp == 8 and at == [D, D, D] and NC == 4
    z = types.SimpleNamespace(n_dp=n_dp, R=R, S=S, D=D, L=L, F=F, heads=heads, in_kernel=in_kernel, QB=QB, KW=KW, TR=32,
                              unroll=4, jobs=jobs, rx_at=rx_at, order=order, pool=POOL)
    ins = dict(lengths=lengths, send_slot=send_slot, recv_place=recv_place, b_query=b_query, b_value=b_value,
               output_bias=output_bias, first_norm_gain=first_norm_gain, first_norm_bias=first_norm_bias, b_up=b_up,
               down_bias=down_bias, second_norm_gain=second_norm_gain, second_norm_bias=second_norm_bias,
               tokens=tokens, wq=w_query.T, wk=w_key.T, wv=w_value.T, wo=w_out, wu=w_up, wd=w_down, og=out_grad)
    any_, vmem, smem = (pl.BlockSpec(memory_space=m) for m in (pl.ANY, pltpu.VMEM, pltpu.SMEM))
    in_specs = [smem] * 3 + [vmem] * 9 + [any_] * 8
    outs = dict(
        res=((T, D), BF16), tg=((T, D), F32), gsum=((3, D, D), BF16), vt=((16, D // 2), BF16), loss_v=((8, 128), F32)
    )
    V = pltpu.VMEM
    dma = pltpu.SemaphoreType.DMA
    scratch = dict(
        tokens_v=V((T, D), BF16), og_v=V((T, D), BF16), wq_v=V((L, D), BF16), wk_v=V((L, D), BF16),
        wv_v=V((L, D), BF16), wo_all=V((4, L, D), BF16), ctx_all=V((NC, 4, half, L), BF16), wu_v=V((D, F), BF16), wd_v=V((F, D), BF16), vecs=V((9, D), F32),
        q=V((T, L), BF16), k=V((T, L), BF16), v=V((T, L), BF16), ctx=V((T, L), BF16),
        dq=V((T, L), BF16), dk=V((T, L), BF16), dv=V((T, L), BF16), dk_acc=V((R, S, L), F32), dv_acc=V((R, S, L), F32),
        probs=V((NC * heads, QB, KW), BF16),
        xhat1=V((NC, half, D), F32), xhat2=V((NC, half, D), F32), hid=V((NC, half, D), F32), d2=V((NC, half, D), F32),
        d1=V((NC, half, D), F32), rstd1=V((NC, half, 1), F32), rstd2=V((NC, half, 1), F32),
        rest=V((half, D), BF16), dtok=V((half, D), F32),
        hl=V((T, D), BF16), act=V((T, F), BF16), gp=V((T, F), BF16), d2l=V((T, D), BF16), dup=V((T, F), BF16),
        d1l=V((T, D), BF16),
        part=V((2, NC, QB, D), BF16), arecv=V((2, NC, half, D), BF16),
        ysend=V((2, NC, half, D), BF16), yrecv=V((2, NC, half, D), BF16),
        pool=V((16, D), F32), pool_r=V((16, D), F32), dpool=V((16, D), F32), acc=V((9, 8, D), F32),
        outg=V((n_dp * 16, 128), BF16), inc=V((n_dp * 16, 128), BF16), outg2=V((n_dp * 16, 128), BF16),
        inc2=V((n_dp * 16, 128), BF16),
        vmine=V((8, D), F32), vsib=V((8, D), F32), vg=V((16, D // 2), BF16), vr=V((3, 16, D // 2), BF16),
        grad=V((3, D, D), BF16), rx=V((rx_rows, D), BF16),
        in_sem=dma((8,)), w_r=dma((3,)), cx_r=dma((NC, 3)), a_r=dma((2, NC)), y_r=dma((2, NC)),
        g_r=dma((3, NC)), pool_sem=dma((2,)), s_pool=dma((POOL,)), p_r=dma((2, n_dp)),
        v_s=dma((2,)), v_r=dma((3,)), d_r=dma((n_jobs, 4)),
    )
    names = tuple(ins) + tuple(outs) + tuple(scratch)
    res, tg, grads, vec, loss = pl.pallas_call(
        functools.partial(layer_kernel, z, names),
        out_shape=[V(*s) for s in outs.values()],
        in_specs=in_specs,
        out_specs=[vmem] * 5,
        scratch_shapes=list(scratch.values()),
        compiler_params=pltpu.CompilerParams(
            collective_id=0, has_side_effects=True, vmem_limit_bytes=VMEM1
        ),
    )(*ins.values())
    if not z.in_kernel:
        grads, vec = lax.psum((grads, vec), "dp")
    un_outs = [((F, D), F32), ((D, F), F32), ((T, D), BF16), ((T, D), F32)] + [((L, D), F32)] * 4
    n_big = len(un_outs)
    un_outs += [((D,), F32)] * 7 + [((L,), F32)] * 2 + [((R * 3,), F32)]
    o = pl.pallas_call(
        functools.partial(unpack_kernel, z),
        out_shape=[jax.ShapeDtypeStruct(*s) for s in un_outs],
        in_specs=[vmem] * 5,
        out_specs=[any_] * n_big + [vmem] * (len(un_outs) - n_big),
        scratch_shapes=[V((3, D, D), F32), dma((6 + 3 * (D // L),))],
        compiler_params=pltpu.CompilerParams(vmem_limit_bytes=24 * 2**20),
    )(grads, res, tg, vec, loss)
    gd, gu, res, tg, gq, gk, gv, go, v0, v1, v2, v3, v4, v5, v6, bq, bv, loss = o
    return res, loss, tg, gq.T, bq, gk.T, gv.T, bv, go, v0, v1, v2, gu, v6, gd, v3, v4, v5


def solution(mesh):
    rows, flat, cut = P("dp", None), P("dp"), P("mp")
    across, down = P(None, "mp"), P("mp", None)
    return jax.shard_map(
        functools.partial(on_device, mesh.shape["dp"]),
        mesh=mesh,
        in_specs=(rows, rows, flat, flat, across, cut, across, across, cut, down, P(), P(), P(), across, cut, down,
                  P(), P(), P(), rows),
        out_specs=(rows, flat, rows, across, cut, across, across, cut, down, P(), P(), P(), across, cut, down, P(),
                   P(), P()),
        check_vma=False,
    )
```
